32 devices in a mesh: row: 4 (over z), col: 2 (over y), seq: 4 (over x, core).
Axes of the slice: x: 2, y: 2, z: 4, core: 2. Of those that a mesh axis runs over, the one named last changes fastest.
Arguments:
- motion_ids: int32 [384], P('col'), may hold values from 0 to 511
- audio_ids: int32 [384], P('col'), may hold values from 0 to 1023
- segment_ids: int32 [384], replicated, may hold values from 0 to 3, never falling along the last dimension, each value on 1 to 192 neighbouring positions
- motion_table: bfloat16 [512, 8192], P(None, ('row', 'seq')), may hold values from -40 to 40
- audio_table: bfloat16 [1024, 8192], P(None, ('row', 'seq')), may hold values from -40 to 40
- norm_gain: float32 [8192], P(('row', 'seq')), may hold values from 0.5 to 1.5
- w_query: bfloat16 [8192, 8192], P(('row', 'seq'), 'col'), may hold values from -0.1875 to 0.1875
- w_key: bfloat16 [8192, 1024], P(('row', 'seq'), 'col'), may hold values from -0.0625 to 0.0625
- w_value: bfloat16 [8192, 1024], P(('row', 'seq'), 'col'), may hold values from -0.0625 to 0.0625
- w_out: bfloat16 [8192, 8192], P('col', ('row', 'seq')), may hold values from -0.0625 to 0.0625
- out_grad: bfloat16 [384, 8192], P('col', ('row', 'seq')), may hold values from -6 to 6
Outputs:
- layer_out: bfloat16 [384, 8192], P('col', ('row', 'seq'))
- grad_input: bfloat16 [384, 8192], P('col', ('row', 'seq'))
- grad_gain: float32 [8192], P(('row', 'seq'))
- grad_wq: float32 [8192, 8192], P(('row', 'seq'), 'col')
- grad_wk: float32 [8192, 1024], P(('row', 'seq'), 'col')
- grad_wv: float32 [8192, 1024], P(('row', 'seq'), 'col')
- grad_wo: float32 [8192, 8192], P('col', ('row', 'seq'))
The draws below stay inside these ranges and needn't reach their ends.
Inputs may be any that keep to these rules, and one draw needn't show every extreme that they name: `segment_ids`: document ids never fall along the sequence; no document is longer than 192 positions, and one is exactly that long.
All inputs are finite; a program needn't handle non-finite values.
Results may differ from the reference program's by a relative error of at most 0.023.
Values may be sent and summed in bfloat16 or wider, within the bound.
A program may use at most 128 MiB of HBM per device.

```python
import math
from functools import partial
import jax
import jax.numpy as jnp
import numpy as np
from jax import lax

D = 8192
H = 64
KV = 8
HD = 128
VM = 512
VA = 1024
L = 384
KVD = 1024


def table_values(key, row_total, col_total):
    key_base, key_cols, key_rows = jax.random.split(key, 3)
    col_place = jnp.arange(col_total, dtype=jnp.float32) / (col_total - 1)
    values = jnp.clip(jax.random.normal(key_base, (row_total, col_total), jnp.float32), -4.0, 4.0)
    ramp_scale = jnp.exp(jnp.log(3.0) * col_place) / 1.7
    col_scale = ramp_scale * jnp.exp(jax.random.uniform(key_cols, (col_total,), jnp.float32, 0.0, jnp.log(3.3))) / 1.8
    row_scale = jnp.exp(jax.random.uniform(key_rows, (row_total, 1), jnp.float32, jnp.log(0.3), jnp.log(3.0)))
    return (values * col_scale[None, :] * row_scale).astype(jnp.bfloat16)


def draw_motion_table(key, part):
    return table_values(jax.random.fold_in(key, 11), VM, D)


def draw_audio_table(key, part):
    return table_values(jax.random.fold_in(key, 23), VA, D)


def plant(values, key, least, top_value):
    longest = values.shape.index(max(values.shape))
    spots = []
    for shift in (0, 1):
        where = [jax.random.randint(jax.random.fold_in(key, axis), (), 0, length) for axis, length in enumerate(values.shape)]
        where[longest] = (where[longest] + shift) % values.shape[longest]
        spots.append(tuple(where))
    return values.at[spots[0]].set(least).at[spots[1]].set(top_value)


def block_scale(key, extent, cuts, smallest, largest):
    factor_of, own = 1.0, jax.random.fold_in(key, 6)
    for axis_at, blocks in cuts:
        draws = jnp.exp(jax.random.uniform(jax.random.fold_in(own, axis_at), (blocks,), jnp.float32, smallest / len(cuts), largest / len(cuts)))
        factor_of = factor_of * jnp.repeat(draws, extent[axis_at] // blocks).reshape([-1 if axis == axis_at else 1 for axis in range(len(extent))])
    return factor_of


def rank_bounds(number_of, slope):
    loads = [(1 << 20) // math.isqrt(grade ** slope) + 1 for grade in range(1, number_of + 1)]
    spread = 1 + sum(loads) // (1 << 30)
    return np.cumsum(np.array([max(1, weight // spread) for weight in loads]))


def ranked(stream_key, dims, number_of, skew):
    listing = rank_bounds(number_of, skew)
    pick = jax.random.randint(jax.random.fold_in(stream_key, 1), dims, 0, int(listing[number_of - 1]))
    standing = jnp.searchsorted(jnp.asarray(listing, jnp.int32), pick, side="right")
    return jax.random.permutation(jax.random.fold_in(stream_key, 2), number_of)[standing].astype(jnp.int32)


def split_up(count, total, limit, lean):
    loads = [(1 << 20) // math.isqrt(standing ** lean) + 1 for standing in range(2, count + 1)]
    rest, given = total - limit - (count - 1), [1] * (count - 1)
    while rest > 0:
        free = [i for i in range(count - 1) if given[i] < limit]
        whole, left = sum([loads[i] for i in free]), rest
        for i in free:
            extra = min(limit - given[i], max(1, left * loads[i] // whole), rest)
            given[i] = given[i] + extra
            rest = rest - extra
    return np.array([limit] + given)


def uneven_parts(own_key, count, total, reach, skew):
    if count == 2:
        one = jax.random.randint(own_key, (), max(1, total - reach), min(reach, total - 1) + 1)
        return jnp.stack([one, total - one])
    sizes = jnp.asarray(split_up(count, total, reach, skew), jnp.int32)
    pairs = (count - 1) // 2
    source_of, sink = sizes[1:1 + 2 * pairs:2], sizes[2:2 + 2 * pairs:2]
    room = jnp.minimum(source_of - 1, reach - sink)
    moved = jax.random.randint(jax.random.fold_in(own_key, 1), (pairs,), 0, 1 << 20) % (room + 1)
    sizes = sizes.at[1:1 + 2 * pairs:2].set(source_of - moved).at[2:2 + 2 * pairs:2].set(sink + moved)
    return sizes[jax.random.permutation(jax.random.fold_in(own_key, 2), count)]


def gaussian(own_key, dims, deviation, most, cuts=(), kind=jnp.bfloat16):
    entries = deviation * jax.random.normal(own_key, dims, jnp.float32)
    if cuts:
        entries = entries * block_scale(own_key, dims, cuts, -0.22, 0.18)
    return jnp.clip(entries, -most, most).astype(kind)


def setup_inputs(seed: int = 0) -> dict:
    key_list = jax.random.split(jax.random.key(seed), 12)
    motion_ids = plant(ranked(key_list[0], (L,), VM, 2), jax.random.fold_in(key_list[0], 3), 0, VM - 1).astype(jnp.int32)
    audio_ids = plant(ranked(key_list[1], (L,), VA, 2), jax.random.fold_in(key_list[1], 3), 0, VA - 1).astype(jnp.int32)
    segment_ids = jnp.searchsorted(jnp.cumsum(uneven_parts(key_list[2], 4, L, L // 2, 0)), jnp.arange(L), side="right").astype(jnp.int32)
    motion_table = draw_motion_table(jax.random.fold_in(key_list[11], 71), 0)
    audio_table = draw_audio_table(jax.random.fold_in(key_list[11], 71), 0)
    norm_gain = jnp.clip(1.0 + 0.1 * jax.random.normal(key_list[5], (D,), jnp.float32), 0.5, 1.5)
    w_query = gaussian(key_list[6], (D, D), (D // 9) ** -0.5, 0.1875, ((0, 16), (1, 2)))
    w_key = gaussian(key_list[7], (D, KVD), D ** -0.5, 0.0625, ((0, 16), (1, 2)))
    w_value = gaussian(key_list[8], (D, KVD), D ** -0.5, 0.0625, ((0, 16), (1, 2)))
    w_out = gaussian(key_list[9], (D, D), D ** -0.5, 0.0625, ((0, 2), (1, 16)))
    out_grad = gaussian(key_list[10], (L, D), 1.0, 6.0, ((0, 2), (1, 16)))
    return dict(motion_ids=motion_ids, audio_ids=audio_ids, segment_ids=segment_ids, motion_table=motion_table, audio_table=audio_table, norm_gain=norm_gain, w_query=w_query, w_key=w_key, w_value=w_value, w_out=w_out, out_grad=out_grad)


epsilon = 1e-05
softcap = 20.0
rope_base = 500000.0

def rotary_tables(positions, head_size):
    half_size = head_size // 2
    frequency = rope_base ** (-(jnp.arange(half_size, dtype=jnp.float32) * 2.0) / head_size)
    angles = positions.astype(jnp.float32)[:, None] * frequency[None, :]
    return (jnp.cos(angles), jnp.sin(angles))

def rotate_pairs(values, cosines, sines):
    half_size = values.shape[-1] // 2
    first_half = values[..., :half_size]
    second_half = values[..., half_size:]
    cos_part = cosines[:, None, :]
    sin_part = sines[:, None, :]
    return jnp.concatenate([first_half * cos_part - second_half * sin_part, second_half * cos_part + first_half * sin_part], axis=-1)

def rotate_back(values, cosines, sines):
    half_size = values.shape[-1] // 2
    first_half = values[..., :half_size]
    second_half = values[..., half_size:]
    cos_part = cosines[:, None, :]
    sin_part = sines[:, None, :]
    return jnp.concatenate([first_half * cos_part + second_half * sin_part, second_half * cos_part - first_half * sin_part], axis=-1)

def group_pass(allowed, operands):
    query_grp, key_grp, value_grp, dout_grp = operands
    query_full = query_grp.astype(jnp.float32)
    key_full = key_grp.astype(jnp.float32)
    value_full = value_grp.astype(jnp.float32)
    dout_full = dout_grp.astype(jnp.float32)
    score_scale = HD ** (-0.5)
    raw_scores = jnp.einsum('qhd,kd->hqk', query_full, key_full) * score_scale
    capped = softcap * jnp.tanh(raw_scores / softcap)
    weights = jnp.where(allowed[None], jnp.exp(capped), 0.0)
    totals = lax.optimization_barrier(jnp.sum(weights, axis=2))
    weights_round = lax.optimization_barrier(weights.astype(jnp.bfloat16)).astype(jnp.float32)
    attended = jnp.einsum('hqk,kd->qhd', weights_round, value_full)
    attn_out = (attended / totals.T[:, :, None]).astype(jnp.bfloat16)
    attn_probs = weights / totals[:, :, None]
    prob_grads = jnp.einsum('qhd,kd->hqk', dout_full, value_full)
    row_dots = lax.optimization_barrier(jnp.sum(attn_probs * prob_grads, axis=2, keepdims=True))
    grad_scores = (attn_probs * (prob_grads - row_dots) * (1.0 - (capped / softcap) ** 2) * score_scale).astype(jnp.bfloat16)
    grad_scores = lax.optimization_barrier(grad_scores).astype(jnp.float32)
    probs_round = lax.optimization_barrier(attn_probs.astype(jnp.bfloat16)).astype(jnp.float32)
    grad_query = jnp.einsum('hqk,kd->qhd', grad_scores, key_full)
    grad_key = jnp.einsum('hqk,qhd->kd', grad_scores, query_full)
    grad_value = jnp.einsum('hqk,qhd->kd', probs_round, dout_full)
    return (attn_out, grad_query, grad_key, grad_value)

def reference(motion_ids, audio_ids, segment_ids, motion_table, audio_table, norm_gain, w_query, w_key, w_value, w_out, out_grad):
    seq_len = segment_ids.shape[0]
    group_size = H // KV
    embedded = (jnp.take(motion_table, motion_ids, axis=0).astype(jnp.float32) + jnp.take(audio_table, audio_ids, axis=0).astype(jnp.float32)).astype(jnp.bfloat16)
    residual = embedded.astype(jnp.float32)
    inverse = lax.rsqrt(lax.optimization_barrier(jnp.sum(residual * residual, axis=1)) / D + epsilon)
    normed = (residual * inverse[:, None] * norm_gain[None, :]).astype(jnp.bfloat16)
    positions = jnp.arange(seq_len, dtype=jnp.int32)
    cosines, sines = rotary_tables(positions, HD)
    queries = rotate_pairs(jnp.dot(normed, w_query, preferred_element_type=jnp.float32).reshape(seq_len, H, HD), cosines, sines).astype(jnp.bfloat16)
    key_heads = rotate_pairs(jnp.dot(normed, w_key, preferred_element_type=jnp.float32).reshape(seq_len, KV, HD), cosines, sines).astype(jnp.bfloat16)
    value_heads = jnp.dot(normed, w_value, preferred_element_type=jnp.float32).reshape(seq_len, KV, HD).astype(jnp.bfloat16)
    out_heads = jnp.dot(out_grad, w_out.T, preferred_element_type=jnp.float32).astype(jnp.bfloat16).reshape(seq_len, KV, group_size, HD)
    allowed = (positions[None, :] <= positions[:, None]) & (segment_ids[None, :] == segment_ids[:, None])
    stacked = (queries.reshape(seq_len, KV, group_size, HD).transpose(1, 0, 2, 3), key_heads.transpose(1, 0, 2), value_heads.transpose(1, 0, 2), out_heads.transpose(1, 0, 2, 3))
    attn_out, grad_query, grad_key, grad_value = lax.map(partial(group_pass, allowed), stacked)
    attended = attn_out.transpose(1, 0, 2, 3).reshape(seq_len, D)
    grad_query = rotate_back(grad_query.transpose(1, 0, 2, 3).reshape(seq_len, H, HD), cosines, sines).reshape(seq_len, D).astype(jnp.bfloat16)
    grad_key = rotate_back(grad_key.transpose(1, 0, 2), cosines, sines).reshape(seq_len, KV * HD).astype(jnp.bfloat16)
    grad_value = grad_value.transpose(1, 0, 2).reshape(seq_len, KV * HD).astype(jnp.bfloat16)
    layer_out = (residual + jnp.dot(attended, w_out, preferred_element_type=jnp.float32)).astype(jnp.bfloat16)
    grad_wo = jnp.dot(attended.T, out_grad, preferred_element_type=jnp.float32)
    grad_wq = jnp.dot(normed.T, grad_query, preferred_element_type=jnp.float32)
    grad_wk = jnp.dot(normed.T, grad_key, preferred_element_type=jnp.float32)
    grad_wv = jnp.dot(normed.T, grad_value, preferred_element_type=jnp.float32)
    grad_normed = jnp.dot(grad_query, w_query.T, preferred_element_type=jnp.float32) + jnp.dot(grad_key, w_key.T, preferred_element_type=jnp.float32) + jnp.dot(grad_value, w_value.T, preferred_element_type=jnp.float32)
    scaled_grad = grad_normed * norm_gain[None, :]
    total_dot = lax.optimization_barrier(jnp.sum(scaled_grad * residual, axis=1))
    grad_input = (out_grad.astype(jnp.float32) + inverse[:, None] * scaled_grad - residual * (inverse ** 3 * total_dot / D)[:, None]).astype(jnp.bfloat16)
    grad_gain = lax.optimization_barrier(jnp.sum(grad_normed * residual * inverse[:, None], axis=0))
    return (layer_out, grad_input, grad_gain, grad_wq, grad_wk, grad_wv, grad_wo)
```

```python
import jax
import jax.numpy as jnp
from jax import lax
from jax.sharding import PartitionSpec as P

D = 8192
H = 64
KV = 8
HD = 128


epsilon = 1e-05
softcap = 20.0
rope_base = 500000.0


def rotary_tables(positions, head_size):
    half_size = head_size // 2
    frequency = rope_base ** (-(jnp.arange(half_size, dtype=jnp.float32) * 2.0) / head_size)
    angles = positions.astype(jnp.float32)[:, None] * frequency[None, :]
    return (jnp.cos(angles), jnp.sin(angles))


def rotate_pairs(values, cosines, sines):
    half_size = values.shape[-1] // 2
    first_half = values[..., :half_size]
    second_half = values[..., half_size:]
    cos_part = cosines[:, None, :]
    sin_part = sines[:, None, :]
    return jnp.concatenate(
        [
            first_half * cos_part - second_half * sin_part,
            second_half * cos_part + first_half * sin_part,
        ],
        axis=-1,
    )


def rotate_back(values, cosines, sines):
    half_size = values.shape[-1] // 2
    first_half = values[..., :half_size]
    second_half = values[..., half_size:]
    cos_part = cosines[:, None, :]
    sin_part = sines[:, None, :]
    return jnp.concatenate(
        [
            first_half * cos_part + second_half * sin_part,
            second_half * cos_part - first_half * sin_part,
        ],
        axis=-1,
    )


def rope_round(values, positions):
    cosines, sines = rotary_tables(positions, HD)
    row_total = values.shape[0]
    return (
        rotate_pairs(values.reshape(row_total, -1, HD), cosines, sines)
        .reshape(row_total, -1)
        .astype(jnp.bfloat16)
    )


def plain_round(values, positions):
    return values.astype(jnp.bfloat16)


def general_device(
    motion_ids,
    audio_ids,
    segment_ids,
    motion_table,
    audio_table,
    norm_gain,
    w_query,
    w_key,
    w_value,
    w_out,
    out_grad,
):
    seq_len = segment_ids.shape[0]
    row_devices = lax.axis_size("row")
    seq_devices = lax.axis_size("seq")
    row_index = lax.axis_index("row")
    seq_index = lax.axis_index("seq")
    col_index = lax.axis_index("col")
    block_len = seq_len // (row_devices * seq_devices)
    quarter_len = seq_len // row_devices
    query_width = w_query.shape[1]
    kv_width = w_key.shape[1]
    heads_col = query_width // HD
    kv_col = kv_width // HD
    group_size = H // KV
    score_scale = HD ** (-0.5)
    block_pos = (row_index * seq_devices + seq_index) * block_len + jnp.arange(
        block_len, dtype=jnp.int32
    )
    embedded = (
        jnp.take(motion_table, motion_ids, axis=0).astype(jnp.float32)
        + jnp.take(audio_table, audio_ids, axis=0).astype(jnp.float32)
    ).astype(jnp.bfloat16)
    residual = embedded.astype(jnp.float32)
    squares = lax.psum(jnp.sum(residual * residual, axis=1), ("row", "seq"))
    inverse = lax.rsqrt(squares / D + epsilon)
    normed = (residual * inverse[:, None] * norm_gain[None, :]).astype(jnp.bfloat16)
    normed_all = lax.all_gather(normed, "col", axis=0, tiled=True)
    query_pos = row_index * quarter_len + jnp.arange(quarter_len, dtype=jnp.int32)
    head_first = col_index * heads_col + seq_index * (heads_col // seq_devices)
    head_count = heads_col // seq_devices

    def to_heads(term, finish):
        own_share = lax.psum_scatter(
            term(jnp.int32(0), block_len * lax.axis_size(("row", "seq"))),
            ("row", "seq"),
            scatter_dimension=0,
            tiled=True,
        )
        return lax.all_to_all(
            finish(own_share, block_pos), "seq", split_axis=1, concat_axis=0, tiled=True
        )

    def to_rows(heads_part):
        own_share = lax.all_to_all(heads_part, "seq", split_axis=0, concat_axis=1, tiled=True)
        return lax.all_gather(own_share, ("row", "seq"), axis=0, tiled=True)

    def query_term(first_row, row_count):
        return jnp.dot(normed_all, w_query, preferred_element_type=jnp.float32)

    queries = to_heads(query_term, rope_round)
    picked = normed_all
    kv_sum = lax.psum_scatter(
        jnp.concatenate(
            [
                jnp.dot(picked, w_key, preferred_element_type=jnp.float32),
                jnp.dot(picked, w_value, preferred_element_type=jnp.float32),
            ],
            axis=1,
        ),
        ("row", "seq"),
        scatter_dimension=0,
        tiled=True,
    )
    kv_block = jnp.concatenate(
        [rope_round(kv_sum[:, :kv_width], block_pos), kv_sum[:, kv_width:].astype(jnp.bfloat16)],
        axis=1,
    )
    kv_all = lax.all_gather(kv_block, ("row", "seq"), axis=0, tiled=True)
    query_len = queries.shape[0]
    kv_slot = (
        head_first + jnp.arange(head_count, dtype=jnp.int32)
    ) // group_size - col_index * kv_col
    key_sel = jnp.take(kv_all[:, :kv_width].reshape(seq_len, kv_col, HD), kv_slot, axis=1)
    value_sel = jnp.take(kv_all[:, kv_width:].reshape(seq_len, kv_col, HD), kv_slot, axis=1)
    key_pos = jnp.arange(seq_len, dtype=jnp.int32)
    allowed = (key_pos[None, :] <= query_pos[:, None]) & (
        segment_ids[None, :] == jnp.take(segment_ids, query_pos)[:, None]
    )
    query_heads = queries.reshape(query_len, head_count, HD)
    raw_scores = (
        jnp.einsum("qhd,khd->hqk", query_heads, key_sel, preferred_element_type=jnp.float32)
        * score_scale
    )
    capped = softcap * jnp.tanh(raw_scores / softcap)
    weights = jnp.where(allowed[None], jnp.exp(capped), 0.0)
    totals = jnp.sum(weights, axis=2)
    attended = jnp.einsum(
        "hqk,khd->qhd", weights.astype(jnp.bfloat16), value_sel, preferred_element_type=jnp.float32
    )
    attn_out = (
        (attended / totals.T[:, :, None]).astype(jnp.bfloat16).reshape(query_len, head_count * HD)
    )
    out_all = to_rows(attn_out)
    picked = out_all
    branch_sum = lax.psum_scatter(
        jnp.dot(picked, w_out, preferred_element_type=jnp.float32).astype(jnp.bfloat16),
        "col",
        scatter_dimension=0,
        tiled=True,
    ).astype(jnp.float32)
    layer_out = (residual + branch_sum).astype(jnp.bfloat16)
    grad_all = lax.all_gather(out_grad, "col", axis=0, tiled=True)
    grad_wo = jnp.einsum("ln,ld->nd", out_all, grad_all, preferred_element_type=jnp.float32)

    def dout_term(first_row, row_count):
        return jnp.einsum("ld,nd->ln", grad_all, w_out, preferred_element_type=jnp.float32)

    out_heads = to_heads(dout_term, plain_round).reshape(query_len, head_count, HD)
    attn_probs = weights / totals[:, :, None]
    prob_grads = jnp.einsum(
        "qhd,khd->hqk", out_heads, value_sel, preferred_element_type=jnp.float32
    )
    row_dots = jnp.sum(attn_probs * prob_grads, axis=2, keepdims=True)
    grad_scores = (
        attn_probs * (prob_grads - row_dots) * (1.0 - (capped / softcap) ** 2) * score_scale
    ).astype(jnp.bfloat16)
    grad_query = jnp.einsum(
        "hqk,khd->qhd", grad_scores, key_sel, preferred_element_type=jnp.float32
    )
    grad_key_heads = jnp.einsum(
        "hqk,qhd->khd", grad_scores, query_heads, preferred_element_type=jnp.float32
    )
    grad_value_heads = jnp.einsum(
        "hqk,qhd->khd",
        attn_probs.astype(jnp.bfloat16),
        out_heads,
        preferred_element_type=jnp.float32,
    )
    slot_mask = (kv_slot[:, None] == jnp.arange(kv_col, dtype=jnp.int32)[None, :]).astype(
        jnp.float32
    )
    grad_key_part = jnp.sum(
        grad_key_heads[:, :, None, :] * slot_mask[None, :, :, None], axis=1
    ).reshape(seq_len, kv_width)
    grad_value_part = jnp.sum(
        grad_value_heads[:, :, None, :] * slot_mask[None, :, :, None], axis=1
    ).reshape(seq_len, kv_width)
    kv_grad_sum = lax.psum_scatter(
        jnp.concatenate([grad_key_part, grad_value_part], axis=1).astype(jnp.bfloat16),
        ("row", "seq"),
        scatter_dimension=0,
        tiled=True,
    ).astype(jnp.float32)
    cos_block, sin_block = rotary_tables(block_pos, HD)
    grad_key_block = (
        rotate_back(kv_grad_sum[:, :kv_width].reshape(block_len, kv_col, HD), cos_block, sin_block)
        .reshape(block_len, kv_width)
        .astype(jnp.bfloat16)
    )
    kv_grad_block = jnp.concatenate(
        [grad_key_block, kv_grad_sum[:, kv_width:].astype(jnp.bfloat16)], axis=1
    )
    kv_grad_all = lax.all_gather(kv_grad_block, ("row", "seq"), axis=0, tiled=True)
    cos_query, sin_query = rotary_tables(query_pos, HD)
    grad_query_round = (
        rotate_back(grad_query, cos_query, sin_query)
        .reshape(query_len, head_count * HD)
        .astype(jnp.bfloat16)
    )
    grad_query_all = to_rows(grad_query_round)
    grad_wq = jnp.einsum(
        "ld,ln->dn", normed_all, grad_query_all, preferred_element_type=jnp.float32
    )
    grad_wk = jnp.einsum(
        "ld,ln->dn", normed_all, kv_grad_all[:, :kv_width], preferred_element_type=jnp.float32
    )
    grad_wv = jnp.einsum(
        "ld,ln->dn", normed_all, kv_grad_all[:, kv_width:], preferred_element_type=jnp.float32
    )
    total_term = jnp.einsum(
        "ln,dn->ld", grad_query_all, w_query, preferred_element_type=jnp.float32
    )
    total_term = total_term + jnp.einsum(
        "ln,dn->ld", kv_grad_all[:, :kv_width], w_key, preferred_element_type=jnp.float32
    )
    grad_normed = lax.psum_scatter(
        (
            total_term
            + jnp.einsum(
                "ln,dn->ld", kv_grad_all[:, kv_width:], w_value, preferred_element_type=jnp.float32
            )
        ).astype(jnp.bfloat16),
        "col",
        scatter_dimension=0,
        tiled=True,
    ).astype(jnp.float32)
    scaled_grad = grad_normed * norm_gain[None, :]
    total_dot = lax.psum(jnp.sum(scaled_grad * residual, axis=1), ("row", "seq"))
    grad_input = (
        out_grad.astype(jnp.float32)
        + inverse[:, None] * scaled_grad
        - residual * (inverse**3 * total_dot / D)[:, None]
    ).astype(jnp.bfloat16)
    grad_gain = lax.psum(jnp.sum(grad_normed * residual * inverse[:, None], axis=0), "col")
    return (layer_out, grad_input, grad_gain, grad_wq, grad_wk, grad_wv, grad_wo)


def fast_device(
    motion_ids,
    audio_ids,
    segment_ids,
    motion_table,
    audio_table,
    norm_gain,
    w_query,
    w_key,
    w_value,
    w_out,
    out_grad,
):
    f32, bf16 = jnp.float32, jnp.bfloat16
    seq_len = segment_ids.shape[0]
    row_devices = lax.axis_size("row")
    seq_devices = lax.axis_size("seq")
    groups = row_devices * seq_devices
    row_index = lax.axis_index("row")
    seq_index = lax.axis_index("seq")
    col_index = lax.axis_index("col")
    own_len = out_grad.shape[0]
    model_width = out_grad.shape[1]
    query_width = w_query.shape[1]
    kv_width = w_key.shape[1]
    head_count = query_width // HD // groups
    kv_len = seq_len // seq_devices
    score_scale = HD ** (-0.5)

    embedded = (
        jnp.take(motion_table, motion_ids, axis=0).astype(f32)
        + jnp.take(audio_table, audio_ids, axis=0).astype(f32)
    ).astype(bf16)
    both = lax.all_gather(
        jnp.concatenate([embedded, out_grad], axis=1), "col", axis=0, tiled=True
    )
    embedded_all = both[:, :model_width]
    grad_all = both[:, model_width:]
    residual_all = embedded_all.astype(f32)
    squares = lax.psum(jnp.sum(residual_all * residual_all, axis=1), ("row", "seq"))
    inverse = lax.rsqrt(squares / D + epsilon)
    scaled = (residual_all * norm_gain[None, :]).astype(bf16)

    def product(left, right):
        return jnp.dot(left, right, preferred_element_type=f32).astype(bf16)

    kv_part = jnp.concatenate(
        [
            product(scaled, w_key).reshape(seq_len, row_devices, HD),
            product(scaled, w_value).reshape(seq_len, row_devices, HD),
        ],
        axis=2,
    ).reshape(seq_len, 2 * kv_width)
    kv_sum = lax.psum(
        lax.psum_scatter(kv_part, "row", scatter_dimension=1, tiled=True), "seq"
    ).astype(f32)
    query_sum = lax.psum_scatter(
        product(scaled, w_query), ("row", "seq"), scatter_dimension=1, tiled=True
    ).astype(f32)
    out_part = jnp.einsum("ld,nd->ln", grad_all, w_out, preferred_element_type=f32).astype(bf16)
    out_heads = lax.psum_scatter(
        out_part, ("row", "seq"), scatter_dimension=1, tiled=True
    ).reshape(seq_len, head_count, HD)

    positions = jnp.arange(seq_len, dtype=jnp.int32)
    cosines, sines = rotary_tables(positions, HD)
    query_heads = rotate_pairs(
        (query_sum * inverse[:, None]).reshape(seq_len, head_count, HD), cosines, sines
    ).astype(bf16)
    kv_scaled = kv_sum * inverse[:, None]
    keys = rotate_pairs(kv_scaled[:, None, :HD], cosines, sines)[:, 0].astype(bf16)
    values = kv_scaled[:, HD:].astype(bf16)

    allowed = (positions[None, :] <= positions[:, None]) & (
        segment_ids[None, :] == segment_ids[:, None]
    )
    raw_scores = jnp.einsum("qhd,kd->hqk", query_heads, keys, preferred_element_type=f32)
    tanh_scores = jnp.tanh(raw_scores * (score_scale / softcap))
    weights = jnp.where(allowed[None], jnp.exp(softcap * tanh_scores), 0.0)
    totals = jnp.sum(weights, axis=2)
    attended = jnp.einsum(
        "hqk,kd->qhd", weights.astype(bf16), values, preferred_element_type=f32
    )
    attn_out = (attended / totals.T[:, :, None]).astype(bf16).reshape(seq_len, head_count * HD)
    out_all = lax.all_gather(attn_out, ("row", "seq"), axis=1, tiled=True)

    probs = weights / totals[:, :, None]
    prob_grads = jnp.einsum("qhd,kd->hqk", out_heads, values, preferred_element_type=f32)
    row_dots = jnp.sum(probs * prob_grads, axis=2, keepdims=True)
    grad_scores = (
        probs * (prob_grads - row_dots) * (1.0 - tanh_scores**2) * score_scale
    ).astype(bf16)
    grad_query = jnp.einsum("hqk,kd->qhd", grad_scores, keys, preferred_element_type=f32)
    grad_key = jnp.einsum("hqk,qhd->kd", grad_scores, query_heads, preferred_element_type=f32)
    grad_value = jnp.einsum(
        "hqk,qhd->kd", probs.astype(bf16), out_heads, preferred_element_type=f32
    )
    dot_query = jnp.sum(grad_query * query_heads.astype(f32), axis=(1, 2))
    grad_query_own = (
        rotate_back(grad_query, cosines, sines).astype(bf16).reshape(seq_len, head_count * HD)
    )
    kv_first = seq_index * kv_len
    kv_grad = lax.psum_scatter(
        jnp.concatenate([grad_key, grad_value], axis=1).astype(bf16),
        "seq",
        scatter_dimension=0,
        tiled=True,
    ).astype(f32)

    def own_rows(array):
        return lax.dynamic_slice_in_dim(array, kv_first, kv_len, axis=0)

    kv_own = own_rows(jnp.concatenate([keys, values], axis=1)).astype(f32)
    dot_kv = jnp.sum(kv_grad * kv_own, axis=1)
    dot_part = lax.dynamic_update_slice_in_dim(
        dot_query, own_rows(dot_query) + dot_kv, kv_first, axis=0
    )
    grad_key_own = rotate_back(kv_grad[:, None, :HD], own_rows(cosines), own_rows(sines))[:, 0]
    kv_grad_own = jnp.concatenate([grad_key_own, kv_grad[:, HD:]], axis=1).astype(bf16)
    kv_grad_all = lax.all_gather(
        lax.all_gather(kv_grad_own, "seq", axis=0, tiled=True), "row", axis=1, tiled=False
    )
    grad_query_all = lax.all_gather(grad_query_own, ("row", "seq"), axis=1, tiled=True)
    grad_key_all = kv_grad_all[:, :, :HD].reshape(seq_len, kv_width)
    grad_value_all = kv_grad_all[:, :, HD:].reshape(seq_len, kv_width)

    dot_sum = lax.psum(dot_part, ("row", "seq", "col"))
    normed = (residual_all * inverse[:, None] * norm_gain[None, :]).astype(bf16)
    branch_part = product(out_all, w_out)
    grad_wo = jnp.einsum("ln,ld->nd", out_all, grad_all, preferred_element_type=f32)
    grad_wq = jnp.einsum("ld,ln->dn", normed, grad_query_all, preferred_element_type=f32)
    grad_wk = jnp.einsum("ld,ln->dn", normed, grad_key_all, preferred_element_type=f32)
    grad_wv = jnp.einsum("ld,ln->dn", normed, grad_value_all, preferred_element_type=f32)
    normed_part = (
        jnp.einsum("ln,dn->ld", grad_query_all, w_query, preferred_element_type=f32)
        + jnp.einsum("ln,dn->ld", grad_key_all, w_key, preferred_element_type=f32)
        + jnp.einsum("ln,dn->ld", grad_value_all, w_value, preferred_element_type=f32)
    )
    gain_part = jnp.sum(normed_part * residual_all * inverse[:, None], axis=0)
    branch_sum, grad_normed = (
        lax.psum_scatter(
            jnp.concatenate([branch_part, normed_part.astype(bf16)], axis=1),
            "col",
            scatter_dimension=0,
            tiled=True,
        )
        .astype(f32)
        .reshape(own_len, 2, model_width)
        .swapaxes(0, 1)
    )
    grad_gain = lax.psum(gain_part, "col")

    def own_part(array):
        return lax.dynamic_slice_in_dim(array, col_index * own_len, own_len, axis=0)

    residual = embedded.astype(f32)
    inverse_own = own_part(inverse)[:, None]
    layer_out = (residual + branch_sum).astype(bf16)
    grad_input = (
        out_grad.astype(f32)
        + inverse_own * (grad_normed * norm_gain[None, :])
        - residual * (inverse_own**2 * own_part(dot_sum)[:, None] / D)
    ).astype(bf16)
    return (layer_out, grad_input, grad_gain, grad_wq, grad_wk, grad_wv, grad_wo)


def solution(mesh):
    placed = (
        P("col"),
        P("col"),
        P(),
        P(None, ("row", "seq")),
        P(None, ("row", "seq")),
        P(("row", "seq")),
        P(("row", "seq"), "col"),
        P(("row", "seq"), "col"),
        P(("row", "seq"), "col"),
        P("col", ("row", "seq")),
        P("col", ("row", "seq")),
    )
    groups = mesh.shape["row"] * mesh.shape["seq"]
    heads_col = H // mesh.shape["col"]
    whole_heads = (
        heads_col % groups == 0
        and KV // mesh.shape["col"] == mesh.shape["row"]
        and mesh.shape["seq"] == 4
    )
    return jax.shard_map(
        fast_device if whole_heads else general_device,
        mesh=mesh,
        in_specs=placed,
        out_specs=(
            P("col", ("row", "seq")),
            P("col", ("row", "seq")),
            P(("row", "seq")),
            P(("row", "seq"), "col"),
            P(("row", "seq"), "col"),
            P(("row", "seq"), "col"),
            P("col", ("row", "seq")),
        ),
        check_vma=False,
    )
```

```python
import jax
import jax.numpy as jnp
from jax import lax
from jax.experimental import pallas as pl
from jax.experimental.pallas import tpu as pltpu
from jax.sharding import PartitionSpec as P

D = 8192
H = 64
KV = 8
HD = 128


epsilon = 1e-05
softcap = 20.0
rope_base = 500000.0


def rotary_tables(positions, head_size):
    half_size = head_size // 2
    frequency = rope_base ** (-(jnp.arange(half_size, dtype=jnp.float32) * 2.0) / head_size)
    angles = positions.astype(jnp.float32)[:, None] * frequency[None, :]
    return (jnp.cos(angles), jnp.sin(angles))


def rotate_pairs(values, cosines, sines):
    half_size = values.shape[-1] // 2
    first_half = values[..., :half_size]
    second_half = values[..., half_size:]
    cos_part = cosines[:, None, :]
    sin_part = sines[:, None, :]
    return jnp.concatenate(
        [
            first_half * cos_part - second_half * sin_part,
            second_half * cos_part + first_half * sin_part,
        ],
        axis=-1,
    )


def rotate_back(values, cosines, sines):
    half_size = values.shape[-1] // 2
    first_half = values[..., :half_size]
    second_half = values[..., half_size:]
    cos_part = cosines[:, None, :]
    sin_part = sines[:, None, :]
    return jnp.concatenate(
        [
            first_half * cos_part + second_half * sin_part,
            second_half * cos_part - first_half * sin_part,
        ],
        axis=-1,
    )


def rope_round(values, positions):
    cosines, sines = rotary_tables(positions, HD)
    row_total = values.shape[0]
    return (
        rotate_pairs(values.reshape(row_total, -1, HD), cosines, sines)
        .reshape(row_total, -1)
        .astype(jnp.bfloat16)
    )


def plain_round(values, positions):
    return values.astype(jnp.bfloat16)


def general_device(
    motion_ids,
    audio_ids,
    segment_ids,
    motion_table,
    audio_table,
    norm_gain,
    w_query,
    w_key,
    w_value,
    w_out,
    out_grad,
):
    seq_len = segment_ids.shape[0]
    row_devices = lax.axis_size("row")
    seq_devices = lax.axis_size("seq")
    row_index = lax.axis_index("row")
    seq_index = lax.axis_index("seq")
    col_index = lax.axis_index("col")
    block_len = seq_len // (row_devices * seq_devices)
    quarter_len = seq_len // row_devices
    query_width = w_query.shape[1]
    kv_width = w_key.shape[1]
    heads_col = query_width // HD
    kv_col = kv_width // HD
    group_size = H // KV
    score_scale = HD ** (-0.5)
    block_pos = (row_index * seq_devices + seq_index) * block_len + jnp.arange(
        block_len, dtype=jnp.int32
    )
    embedded = (
        jnp.take(motion_table, motion_ids, axis=0).astype(jnp.float32)
        + jnp.take(audio_table, audio_ids, axis=0).astype(jnp.float32)
    ).astype(jnp.bfloat16)
    residual = embedded.astype(jnp.float32)
    squares = lax.psum(jnp.sum(residual * residual, axis=1), ("row", "seq"))
    inverse = lax.rsqrt(squares / D + epsilon)
    normed = (residual * inverse[:, None] * norm_gain[None, :]).astype(jnp.bfloat16)
    normed_all = lax.all_gather(normed, "col", axis=0, tiled=True)
    query_pos = row_index * quarter_len + jnp.arange(quarter_len, dtype=jnp.int32)
    head_first = col_index * heads_col + seq_index * (heads_col // seq_devices)
    head_count = heads_col // seq_devices

    def to_heads(term, finish):
        own_share = lax.psum_scatter(
            term(jnp.int32(0), block_len * lax.axis_size(("row", "seq"))),
            ("row", "seq"),
            scatter_dimension=0,
            tiled=True,
        )
        return lax.all_to_all(
            finish(own_share, block_pos), "seq", split_axis=1, concat_axis=0, tiled=True
        )

    def to_rows(heads_part):
        own_share = lax.all_to_all(heads_part, "seq", split_axis=0, concat_axis=1, tiled=True)
        return lax.all_gather(own_share, ("row", "seq"), axis=0, tiled=True)

    def query_term(first_row, row_count):
        return jnp.dot(normed_all, w_query, preferred_element_type=jnp.float32)

    queries = to_heads(query_term, rope_round)
    picked = normed_all
    kv_sum = lax.psum_scatter(
        jnp.concatenate(
            [
                jnp.dot(picked, w_key, preferred_element_type=jnp.float32),
                jnp.dot(picked, w_value, preferred_element_type=jnp.float32),
            ],
            axis=1,
        ),
        ("row", "seq"),
        scatter_dimension=0,
        tiled=True,
    )
    kv_block = jnp.concatenate(
        [rope_round(kv_sum[:, :kv_width], block_pos), kv_sum[:, kv_width:].astype(jnp.bfloat16)],
        axis=1,
    )
    kv_all = lax.all_gather(kv_block, ("row", "seq"), axis=0, tiled=True)
    query_len = queries.shape[0]
    kv_slot = (
        head_first + jnp.arange(head_count, dtype=jnp.int32)
    ) // group_size - col_index * kv_col
    key_sel = jnp.take(kv_all[:, :kv_width].reshape(seq_len, kv_col, HD), kv_slot, axis=1)
    value_sel = jnp.take(kv_all[:, kv_width:].reshape(seq_len, kv_col, HD), kv_slot, axis=1)
    key_pos = jnp.arange(seq_len, dtype=jnp.int32)
    allowed = (key_pos[None, :] <= query_pos[:, None]) & (
        segment_ids[None, :] == jnp.take(segment_ids, query_pos)[:, None]
    )
    query_heads = queries.reshape(query_len, head_count, HD)
    raw_scores = (
        jnp.einsum("qhd,khd->hqk", query_heads, key_sel, preferred_element_type=jnp.float32)
        * score_scale
    )
    capped = softcap * jnp.tanh(raw_scores / softcap)
    weights = jnp.where(allowed[None], jnp.exp(capped), 0.0)
    totals = jnp.sum(weights, axis=2)
    attended = jnp.einsum(
        "hqk,khd->qhd", weights.astype(jnp.bfloat16), value_sel, preferred_element_type=jnp.float32
    )
    attn_out = (
        (attended / totals.T[:, :, None]).astype(jnp.bfloat16).reshape(query_len, head_count * HD)
    )
    out_all = to_rows(attn_out)
    picked = out_all
    branch_sum = lax.psum_scatter(
        jnp.dot(picked, w_out, preferred_element_type=jnp.float32).astype(jnp.bfloat16),
        "col",
        scatter_dimension=0,
        tiled=True,
    ).astype(jnp.float32)
    layer_out = (residual + branch_sum).astype(jnp.bfloat16)
    grad_all = lax.all_gather(out_grad, "col", axis=0, tiled=True)
    grad_wo = jnp.einsum("ln,ld->nd", out_all, grad_all, preferred_element_type=jnp.float32)

    def dout_term(first_row, row_count):
        return jnp.einsum("ld,nd->ln", grad_all, w_out, preferred_element_type=jnp.float32)

    out_heads = to_heads(dout_term, plain_round).reshape(query_len, head_count, HD)
    attn_probs = weights / totals[:, :, None]
    prob_grads = jnp.einsum(
        "qhd,khd->hqk", out_heads, value_sel, preferred_element_type=jnp.float32
    )
    row_dots = jnp.sum(attn_probs * prob_grads, axis=2, keepdims=True)
    grad_scores = (
        attn_probs * (prob_grads - row_dots) * (1.0 - (capped / softcap) ** 2) * score_scale
    ).astype(jnp.bfloat16)
    grad_query = jnp.einsum(
        "hqk,khd->qhd", grad_scores, key_sel, preferred_element_type=jnp.float32
    )
    grad_key_heads = jnp.einsum(
        "hqk,qhd->khd", grad_scores, query_heads, preferred_element_type=jnp.float32
    )
    grad_value_heads = jnp.einsum(
        "hqk,qhd->khd",
        attn_probs.astype(jnp.bfloat16),
        out_heads,
        preferred_element_type=jnp.float32,
    )
    slot_mask = (kv_slot[:, None] == jnp.arange(kv_col, dtype=jnp.int32)[None, :]).astype(
        jnp.float32
    )
    grad_key_part = jnp.sum(
        grad_key_heads[:, :, None, :] * slot_mask[None, :, :, None], axis=1
    ).reshape(seq_len, kv_width)
    grad_value_part = jnp.sum(
        grad_value_heads[:, :, None, :] * slot_mask[None, :, :, None], axis=1
    ).reshape(seq_len, kv_width)
    kv_grad_sum = lax.psum_scatter(
        jnp.concatenate([grad_key_part, grad_value_part], axis=1).astype(jnp.bfloat16),
        ("row", "seq"),
        scatter_dimension=0,
        tiled=True,
    ).astype(jnp.float32)
    cos_block, sin_block = rotary_tables(block_pos, HD)
    grad_key_block = (
        rotate_back(kv_grad_sum[:, :kv_width].reshape(block_len, kv_col, HD), cos_block, sin_block)
        .reshape(block_len, kv_width)
        .astype(jnp.bfloat16)
    )
    kv_grad_block = jnp.concatenate(
        [grad_key_block, kv_grad_sum[:, kv_width:].astype(jnp.bfloat16)], axis=1
    )
    kv_grad_all = lax.all_gather(kv_grad_block, ("row", "seq"), axis=0, tiled=True)
    cos_query, sin_query = rotary_tables(query_pos, HD)
    grad_query_round = (
        rotate_back(grad_query, cos_query, sin_query)
        .reshape(query_len, head_count * HD)
        .astype(jnp.bfloat16)
    )
    grad_query_all = to_rows(grad_query_round)
    grad_wq = jnp.einsum(
        "ld,ln->dn", normed_all, grad_query_all, preferred_element_type=jnp.float32
    )
    grad_wk = jnp.einsum(
        "ld,ln->dn", normed_all, kv_grad_all[:, :kv_width], preferred_element_type=jnp.float32
    )
    grad_wv = jnp.einsum(
        "ld,ln->dn", normed_all, kv_grad_all[:, kv_width:], preferred_element_type=jnp.float32
    )
    total_term = jnp.einsum(
        "ln,dn->ld", grad_query_all, w_query, preferred_element_type=jnp.float32
    )
    total_term = total_term + jnp.einsum(
        "ln,dn->ld", kv_grad_all[:, :kv_width], w_key, preferred_element_type=jnp.float32
    )
    grad_normed = lax.psum_scatter(
        (
            total_term
            + jnp.einsum(
                "ln,dn->ld", kv_grad_all[:, kv_width:], w_value, preferred_element_type=jnp.float32
            )
        ).astype(jnp.bfloat16),
        "col",
        scatter_dimension=0,
        tiled=True,
    ).astype(jnp.float32)
    scaled_grad = grad_normed * norm_gain[None, :]
    total_dot = lax.psum(jnp.sum(scaled_grad * residual, axis=1), ("row", "seq"))
    grad_input = (
        out_grad.astype(jnp.float32)
        + inverse[:, None] * scaled_grad
        - residual * (inverse**3 * total_dot / D)[:, None]
    ).astype(jnp.bfloat16)
    grad_gain = lax.psum(jnp.sum(grad_normed * residual * inverse[:, None], axis=0), "col")
    return (layer_out, grad_input, grad_gain, grad_wq, grad_wk, grad_wv, grad_wo)


VMEM_BYTES = 56 * 1024 * 1024


def remote(source, target, send_sem, recv_sem, place):
    copy = pltpu.make_async_remote_copy(
        src_ref=source,
        dst_ref=target,
        send_sem=send_sem,
        recv_sem=recv_sem,
        device_id=place,
        device_id_type=pl.DeviceIdType.MESH,
    )
    copy.start()
    return copy


def greet(places):
    barrier = pltpu.get_barrier_semaphore()
    for place in places:
        pl.semaphore_signal(
            barrier, inc=1, device_id=place, device_id_type=pl.DeviceIdType.MESH
        )
    pl.semaphore_wait(barrier, len(places))


def neighbours():
    row = lax.axis_index("row")
    seq = lax.axis_index("seq")
    rows = lax.axis_size("row")
    across, core = seq // 2, seq % 2
    plane = [(across, 1 - core), (1 - across, core), (1 - across, 1 - core)]
    plane_ids = [{"row": row, "seq": 2 * a + c} for a, c in plane]
    plane_slots = [2 * c + a for a, c in plane]
    others = [(row + step) % rows for step in range(1, rows)]
    row_ids = [{"row": other, "seq": seq} for other in others]
    return row, across, core, plane_ids, plane_slots, others, row_ids


def reduce_kernel(
    q_part, o_part, kv_part, sq_part,
    q_out, o_out, kv_out, sq_out,
    q_rc, o_rc, kv_rc, q_a1, o_a1, kv_a1, q_rx, o_rx, kv_rx, q_a2, o_a2, kv_a2,
    q_rz, o_rz, kv_rz, kv_own, kv_all, sq_send, sq_recv,
    core_send, core_recv, x_send, x_recv, z_send, z_recv, kv_send, kv_recv, sq_ss, sq_rs,
):
    f32, bf16 = jnp.float32, jnp.bfloat16
    row, across, core, plane_ids, plane_slots, others, row_ids = neighbours()
    rows = len(others) + 1
    core_id, x_id = plane_ids[0], plane_ids[1]
    greet(plane_ids + row_ids)
    seq_len = q_out.shape[0]
    width = q_out.shape[1]
    block = seq_len // 4
    wide = 2 * width
    half_len = seq_len // 2
    pieces = [(None, 0)] + [(0, b) for b in range(4)] + [(1, b) for b in range(4)]
    parts, rcs, a1s = (q_part, o_part), (q_rc, o_rc), (q_a1, o_a1)
    rxs, a2s, rzs, outs = (q_rx, o_rx), (q_a2, o_a2), (q_rz, o_rz), (q_out, o_out)
    core_copies, x_copies, z_copies = [], [], []

    sq_copy = remote(sq_part, sq_recv.at[0], sq_ss.at[0], sq_rs.at[0], core_id)
    for index, (which, b) in enumerate(pieces):
        copies = []
        if which is None:
            source = kv_part.at[pl.ds(pl.multiple_of((1 - core) * half_len, half_len), half_len)]
            copies.append(
                remote(source, kv_rc, core_send.at[index, 0], core_recv.at[index, 0], core_id)
            )
        else:
            lines = pl.ds(b * block, block)
            for r in range(rows):
                first = pl.multiple_of(r * 2 * wide + (1 - core) * wide, wide)
                copies.append(
                    remote(
                        parts[which].at[lines, pl.ds(first, wide)],
                        rcs[which].at[lines, pl.ds(r * wide, wide)],
                        core_send.at[index, r],
                        core_recv.at[index, r],
                        core_id,
                    )
                )
        core_copies.append(copies)

    def core_stage(index):
        which, b = pieces[index]
        for copy in core_copies[index]:
            copy.wait_recv()
        if which is None:
            own = kv_part[pl.ds(pl.multiple_of(core * half_len, half_len), half_len), :]
            kv_a1[...] = (own.astype(f32) + kv_rc[...].astype(f32)).astype(bf16)
            source = kv_a1.at[pl.ds(pl.multiple_of((1 - across) * block, block), block)]
            target = kv_rx
        else:
            lines = pl.ds(b * block, block)
            for r in range(rows):
                for side in range(2):
                    first = pl.multiple_of(r * 2 * wide + core * wide + side * width, width)
                    total = parts[which][lines, pl.ds(first, width)].astype(f32) + rcs[which][
                        lines, pl.ds(r * wide + side * width, width)
                    ].astype(f32)
                    a1s[which][side, lines, pl.ds(r * width, width)] = total.astype(bf16)
            source = a1s[which].at[1 - across, lines]
            target = rxs[which].at[lines]
        x_copies.append(remote(source, target, x_send.at[index], x_recv.at[index], x_id))

    def x_stage(index):
        which, b = pieces[index]
        x_copies[index].wait_recv()
        lines = pl.ds(b * block, block)
        if which is None:
            held = kv_a1[pl.ds(pl.multiple_of(across * block, block), block), :]
            got, kept, landing, span = kv_rx[...], kv_a2, kv_rz, pl.ds(0, block)
        else:
            held = a1s[which][across, lines, :]
            got, kept, landing, span = rxs[which][lines, :], a2s[which], rzs[which], lines
        total = (held.astype(f32) + got.astype(f32)).astype(bf16)
        for r in range(rows):
            kept[r, span, :] = total[:, r * width : (r + 1) * width]
        z_copies.append(
            [
                remote(
                    kept.at[others[step], span],
                    landing.at[step, span],
                    z_send.at[index, step],
                    z_recv.at[index, step],
                    row_ids[step],
                )
                for step in range(rows - 1)
            ]
        )

    def z_stage(index):
        which, b = pieces[index]
        for copy in z_copies[index]:
            copy.wait_recv()
        lines = pl.ds(b * block, block)
        if which is None:
            kept, landing, span = kv_a2, kv_rz, pl.ds(0, block)
        else:
            kept, landing, span = a2s[which], rzs[which], lines
        total = kept[row, span, :].astype(f32)
        for step in range(rows - 1):
            total = total + landing[step, span, :].astype(f32)
        if which is None:
            kv_own[...] = total
            return [
                remote(
                    kv_own, kv_all.at[step], kv_send.at[step], kv_recv.at[step], plane_ids[step]
                )
                for step in range(3)
            ]
        outs[which][lines, :] = total.astype(outs[which].dtype)
        return []

    kv_copies = []
    sq_copies = [sq_copy]
    for turn in range(len(pieces) + 2):
        if turn < len(pieces):
            core_stage(turn)
        if turn == 1:
            sq_copies[0].wait_recv()
            sq_send[0] = sq_part[...] + sq_recv[0]
            sq_copies.append(
                remote(sq_send.at[0], sq_recv.at[1], sq_ss.at[1], sq_rs.at[1], x_id)
            )
        if turn == 3:
            sq_copies[1].wait_recv()
            sq_send[1] = sq_send[0] + sq_recv[1]
            for step in range(rows - 1):
                sq_copies.append(
                    remote(
                        sq_send.at[1],
                        sq_recv.at[2 + step],
                        sq_ss.at[2 + step],
                        sq_rs.at[2 + step],
                        row_ids[step],
                    )
                )
        if 1 <= turn <= len(pieces):
            x_stage(turn - 1)
        if turn >= 2:
            kv_copies += z_stage(turn - 2)
    total = sq_send[1]
    for step in range(rows - 1):
        sq_copies[2 + step].wait_recv()
        total = total + sq_recv[2 + step]
    sq_out[...] = total
    own_slot = 2 * core + across
    kv_out[pl.ds(pl.multiple_of(own_slot * block, block), block), :] = kv_own[...]
    for step in range(3):
        kv_copies[step].wait_recv()
        first = pl.multiple_of(plane_slots[step] * block, block)
        kv_out[pl.ds(first, block), :] = kv_all[step]
    for copy in sum(core_copies, []) + x_copies + sum(z_copies, []) + kv_copies + sq_copies:
        copy.wait_send()


def reduce_shares(q_part, o_part, kv_part, sq_part, rows):
    f32, bf16 = jnp.float32, jnp.bfloat16
    seq_len, whole = q_part.shape
    width = whole // (4 * rows)
    block = seq_len // 4
    dma = pltpu.SemaphoreType.DMA
    twice = lambda *shape: [pltpu.VMEM(shape, bf16)] * 2
    return pl.pallas_call(
        reduce_kernel,
        out_shape=(
            jax.ShapeDtypeStruct((seq_len, width), f32),
            jax.ShapeDtypeStruct((seq_len, width), bf16),
            jax.ShapeDtypeStruct((seq_len, width), f32),
            jax.ShapeDtypeStruct(sq_part.shape, f32),
        ),
        in_specs=[pl.BlockSpec(memory_space=pltpu.VMEM)] * 4,
        out_specs=[pl.BlockSpec(memory_space=pltpu.VMEM)] * 4,
        scratch_shapes=[
            *twice(seq_len, whole // 2),
            pltpu.VMEM((seq_len // 2, rows * width), bf16),
            *twice(2, seq_len, rows * width),
            pltpu.VMEM((seq_len // 2, rows * width), bf16),
            *twice(seq_len, rows * width),
            pltpu.VMEM((block, rows * width), bf16),
            *twice(rows, seq_len, width),
            pltpu.VMEM((rows, block, width), bf16),
            *twice(rows - 1, seq_len, width),
            pltpu.VMEM((rows - 1, block, width), bf16),
            pltpu.VMEM((block, width), f32),
            pltpu.VMEM((3, block, width), f32),
            pltpu.VMEM((2, *sq_part.shape), f32),
            pltpu.VMEM((1 + rows, *sq_part.shape), f32),
            dma((9, rows)), dma((9, rows)), dma((9,)), dma((9,)),
            dma((9, rows - 1)), dma((9, rows - 1)), dma((3,)), dma((3,)),
            dma((1 + rows,)), dma((1 + rows,)),
        ],
        compiler_params=pltpu.CompilerParams(
            collective_id=0, has_side_effects=True, vmem_limit_bytes=VMEM_BYTES
        ),
    )(q_part, o_part, kv_part, sq_part)


def gather_kernel(
    a_own, q_own, kv_part, cos_ref, sin_ref, dot_part,
    a_all, q_all, kv_all, dot_out,
    kv_recv_buf, dot_send, dot_recv,
    z_send, z_recv, x_send, x_recv, core_send, core_recv,
    r_send, r_recv, kz_send, kz_recv, kp_send, kp_recv, dot_ss, dot_rs,
):
    f32, bf16 = jnp.float32, jnp.bfloat16
    row, across, core, plane_ids, plane_slots, others, row_ids = neighbours()
    rows = len(others) + 1
    core_id, x_id = plane_ids[0], plane_ids[1]
    seq_len, width = a_own.shape
    block = seq_len // 4
    wide = 2 * width
    own_slot = 2 * core + across
    own_first = pl.multiple_of(row * 2 * wide + own_slot * width, width)
    own_lines = pl.ds(pl.multiple_of(own_slot * block, block), block)
    own_kv = pl.ds(pl.multiple_of(row * width, width), width)
    greet(plane_ids + row_ids)

    reduces = []
    for step in range(3):
        first = pl.multiple_of(plane_slots[step] * block, block)
        reduces.append(
            remote(
                kv_part.at[pl.ds(first, block)],
                kv_recv_buf.at[step],
                r_send.at[step],
                r_recv.at[step],
                plane_ids[step],
            )
        )
    dot_copies = [
        remote(dot_part, dot_recv.at[step], dot_ss.at[step], dot_rs.at[step], row_ids[step])
        for step in range(rows - 1)
    ]
    pieces = [(which, b) for which in range(2) for b in range(4)]
    owns, alls = (a_own, q_own), (a_all, q_all)
    z_copies, x_copies, core_copies = [], [], []
    for index, (which, b) in enumerate(pieces):
        lines = pl.ds(b * block, block)
        z_copies.append(
            [
                remote(
                    owns[which].at[lines],
                    alls[which].at[lines, pl.ds(own_first, width)],
                    z_send.at[index, step],
                    z_recv.at[index, step],
                    row_ids[step],
                )
                for step in range(rows - 1)
            ]
        )
    for which in range(2):
        alls[which][:, pl.ds(own_first, width)] = owns[which][...]

    total = kv_part[own_lines, :].astype(f32)
    for step in range(3):
        reduces[step].wait_recv()
        total = total + kv_recv_buf[step].astype(f32)
    head = width // 2
    key_part = total[:, :head]
    cosines, sines = cos_ref[own_lines, :], sin_ref[own_lines, :]
    turned = jnp.concatenate([key_part[:, head // 2 :], key_part[:, : head // 2]], axis=1)
    key_part = key_part * cosines + turned * sines
    kv_all[own_lines, own_kv] = jnp.concatenate([key_part, total[:, head:]], axis=1).astype(bf16)
    kv_z = [
        remote(
            kv_all.at[own_lines, own_kv],
            kv_all.at[own_lines, own_kv],
            kz_send.at[step],
            kz_recv.at[step],
            row_ids[step],
        )
        for step in range(rows - 1)
    ]

    def x_stage(index):
        which, b = pieces[index]
        lines = pl.ds(b * block, block)
        for copy in z_copies[index]:
            copy.wait_recv()
        copies = []
        for r in range(rows):
            first = pl.multiple_of(r * 2 * wide + own_slot * width, width)
            place = alls[which].at[lines, pl.ds(first, width)]
            copies.append(remote(place, place, x_send.at[index, r], x_recv.at[index, r], x_id))
        x_copies.append(copies)

    def core_stage(index):
        which, b = pieces[index]
        lines = pl.ds(b * block, block)
        for copy in x_copies[index]:
            copy.wait_recv()
        copies = []
        for r in range(rows):
            first = pl.multiple_of(r * 2 * wide + core * wide, wide)
            place = alls[which].at[lines, pl.ds(first, wide)]
            copies.append(
                remote(place, place, core_send.at[index, r], core_recv.at[index, r], core_id)
            )
        core_copies.append(copies)

    kv_plane = []
    for turn in range(len(pieces) + 1):
        if turn < len(pieces):
            x_stage(turn)
        if turn == 0:
            total = dot_part[...]
            for step in range(rows - 1):
                dot_copies[step].wait_recv()
                total = total + dot_recv[step]
            dot_send[0] = total
            dot_copies.append(
                remote(
                    dot_send.at[0],
                    dot_recv.at[rows - 1],
                    dot_ss.at[rows - 1],
                    dot_rs.at[rows - 1],
                    x_id,
                )
            )
        if turn == 1:
            for copy in kv_z:
                copy.wait_recv()
            kv_plane = [
                remote(
                    kv_all.at[own_lines],
                    kv_all.at[own_lines],
                    kp_send.at[step],
                    kp_recv.at[step],
                    plane_ids[step],
                )
                for step in range(3)
            ]
        if turn == 2:
            dot_copies[rows - 1].wait_recv()
            dot_send[1] = dot_send[0] + dot_recv[rows - 1]
            dot_copies.append(
                remote(
                    dot_send.at[1], dot_recv.at[rows], dot_ss.at[rows], dot_rs.at[rows], core_id
                )
            )
        if turn >= 1:
            core_stage(turn - 1)
    dot_copies[rows].wait_recv()
    dot_out[...] = dot_send[1] + dot_recv[rows]
    for copy in kv_plane + sum(core_copies, []):
        copy.wait_recv()
    for copy in (
        sum(z_copies + x_copies + core_copies, []) + reduces + kv_z + kv_plane + dot_copies
    ):
        copy.wait_send()


def gather_shares(a_own, q_own, kv_part, cosines, sines, dot_part, rows):
    f32, bf16 = jnp.float32, jnp.bfloat16
    seq_len, width = a_own.shape
    block = seq_len // 4
    whole = width * 4 * rows
    dma = pltpu.SemaphoreType.DMA
    return pl.pallas_call(
        gather_kernel,
        out_shape=(
            jax.ShapeDtypeStruct((seq_len, whole), bf16),
            jax.ShapeDtypeStruct((seq_len, whole), bf16),
            jax.ShapeDtypeStruct((seq_len, rows * width), bf16),
            jax.ShapeDtypeStruct(dot_part.shape, f32),
        ),
        in_specs=[pl.BlockSpec(memory_space=pltpu.VMEM)] * 6,
        out_specs=[pl.BlockSpec(memory_space=pltpu.VMEM)] * 4,
        scratch_shapes=[
            pltpu.VMEM((3, block, width), bf16),
            pltpu.VMEM((2, *dot_part.shape), f32),
            pltpu.VMEM((rows + 1, *dot_part.shape), f32),
            dma((8, rows - 1)), dma((8, rows - 1)), dma((8, rows)), dma((8, rows)),
            dma((8, rows)), dma((8, rows)), dma((3,)), dma((3,)),
            dma((rows - 1,)), dma((rows - 1,)), dma((3,)), dma((3,)),
            dma((rows + 1,)), dma((rows + 1,)),
        ],
        compiler_params=pltpu.CompilerParams(
            collective_id=1, has_side_effects=True, vmem_limit_bytes=VMEM_BYTES
        ),
    )(a_own, q_own, kv_part, cosines, sines, dot_part)


def fast_device(
    motion_ids,
    audio_ids,
    segment_ids,
    motion_table,
    audio_table,
    norm_gain,
    w_query,
    w_key,
    w_value,
    w_out,
    out_grad,
):
    f32, bf16 = jnp.float32, jnp.bfloat16
    seq_len = segment_ids.shape[0]
    row_devices = lax.axis_size("row")
    seq_devices = lax.axis_size("seq")
    groups = row_devices * seq_devices
    col_index = lax.axis_index("col")
    own_len = out_grad.shape[0]
    model_width = out_grad.shape[1]
    query_width = w_query.shape[1]
    kv_width = w_key.shape[1]
    head_count = query_width // HD // groups
    score_scale = HD ** (-0.5)

    embedded = (
        jnp.take(motion_table, motion_ids, axis=0).astype(f32)
        + jnp.take(audio_table, audio_ids, axis=0).astype(f32)
    ).astype(bf16)
    both = lax.all_gather(
        jnp.concatenate([embedded, out_grad], axis=1), "col", axis=0, tiled=True
    )
    embedded_all = both[:, :model_width]
    grad_all = both[:, model_width:]
    residual_all = embedded_all.astype(f32)
    scaled = (residual_all * norm_gain[None, :]).astype(bf16)

    def product(left, right):
        return jnp.dot(left, right, preferred_element_type=f32).astype(bf16)

    def as_rows(vector):
        return jnp.broadcast_to(vector[None, :], (8, seq_len))

    kv_part = jnp.concatenate(
        [
            product(scaled, w_key).reshape(seq_len, row_devices, HD),
            product(scaled, w_value).reshape(seq_len, row_devices, HD),
        ],
        axis=2,
    ).reshape(seq_len, 2 * kv_width)
    out_part = jnp.einsum("ld,nd->ln", grad_all, w_out, preferred_element_type=f32).astype(bf16)
    query_sum, out_heads, kv_sum, squares = reduce_shares(
        product(scaled, w_query),
        out_part,
        kv_part,
        as_rows(jnp.sum(residual_all * residual_all, axis=1)),
        row_devices,
    )
    inverse = lax.rsqrt(squares[0] / D + epsilon)
    out_heads = out_heads.reshape(seq_len, head_count, HD)

    positions = jnp.arange(seq_len, dtype=jnp.int32)
    cosines, sines = rotary_tables(positions, HD)
    query_heads = rotate_pairs(
        (query_sum * inverse[:, None]).reshape(seq_len, head_count, HD), cosines, sines
    ).astype(bf16)
    kv_scaled = kv_sum * inverse[:, None]
    keys = rotate_pairs(kv_scaled[:, None, :HD], cosines, sines)[:, 0].astype(bf16)
    values = kv_scaled[:, HD:].astype(bf16)

    allowed = (positions[None, :] <= positions[:, None]) & (
        segment_ids[None, :] == segment_ids[:, None]
    )
    raw_scores = jnp.einsum("qhd,kd->hqk", query_heads, keys, preferred_element_type=f32)
    tanh_scores = jnp.tanh(raw_scores * (score_scale / softcap))
    weights = jnp.where(allowed[None], jnp.exp(softcap * tanh_scores), 0.0)
    totals = jnp.sum(weights, axis=2)
    attended = jnp.einsum(
        "hqk,kd->qhd", weights.astype(bf16), values, preferred_element_type=f32
    )
    attn_out = (attended / totals.T[:, :, None]).astype(bf16).reshape(seq_len, head_count * HD)
    probs = weights / totals[:, :, None]
    prob_grads = jnp.einsum("qhd,kd->hqk", out_heads, values, preferred_element_type=f32)
    row_dots = jnp.sum(probs * prob_grads, axis=2, keepdims=True)
    grad_scores = (
        probs * (prob_grads - row_dots) * (1.0 - tanh_scores**2) * score_scale
    ).astype(bf16)
    grad_query = jnp.einsum("hqk,kd->qhd", grad_scores, keys, preferred_element_type=f32)
    grad_key = jnp.einsum("hqk,qhd->kd", grad_scores, query_heads, preferred_element_type=f32)
    grad_value = jnp.einsum(
        "hqk,qhd->kd", probs.astype(bf16), out_heads, preferred_element_type=f32
    )
    dot_query = jnp.sum(grad_query * query_heads.astype(f32), axis=(1, 2))
    grad_query_own = (
        rotate_back(grad_query, cosines, sines).astype(bf16).reshape(seq_len, head_count * HD)
    )
    dot_part = dot_query + jnp.sum(
        grad_key * keys.astype(f32) + grad_value * values.astype(f32), axis=1
    )
    out_all, grad_query_all, kv_grad_all, dot_sum = gather_shares(
        attn_out,
        grad_query_own,
        jnp.concatenate([grad_key, grad_value], axis=1).astype(bf16),
        jnp.concatenate([cosines, cosines], axis=1),
        jnp.concatenate([sines, -sines], axis=1),
        as_rows(dot_part),
        row_devices,
    )
    kv_grad_all = kv_grad_all.reshape(seq_len, row_devices, 2 * HD)
    grad_key_all = kv_grad_all[:, :, :HD].reshape(seq_len, kv_width)
    grad_value_all = kv_grad_all[:, :, HD:].reshape(seq_len, kv_width)

    normed = (residual_all * inverse[:, None] * norm_gain[None, :]).astype(bf16)
    branch_part = product(out_all, w_out)
    grad_wo = jnp.einsum("ln,ld->nd", out_all, grad_all, preferred_element_type=f32)
    grad_wq = jnp.einsum("ld,ln->dn", normed, grad_query_all, preferred_element_type=f32)
    grad_wk = jnp.einsum("ld,ln->dn", normed, grad_key_all, preferred_element_type=f32)
    grad_wv = jnp.einsum("ld,ln->dn", normed, grad_value_all, preferred_element_type=f32)
    normed_part = (
        jnp.einsum("ln,dn->ld", grad_query_all, w_query, preferred_element_type=f32)
        + jnp.einsum("ln,dn->ld", grad_key_all, w_key, preferred_element_type=f32)
        + jnp.einsum("ln,dn->ld", grad_value_all, w_value, preferred_element_type=f32)
    )
    gain_part = jnp.sum(normed_part * residual_all * inverse[:, None], axis=0)
    branch_sum, grad_normed = (
        lax.psum_scatter(
            jnp.concatenate([branch_part, normed_part.astype(bf16)], axis=1),
            "col",
            scatter_dimension=0,
            tiled=True,
        )
        .astype(f32)
        .reshape(own_len, 2, model_width)
        .swapaxes(0, 1)
    )
    sums = lax.psum(jnp.concatenate([gain_part, dot_sum[0]]), "col")
    grad_gain, dot_sum = sums[:model_width], sums[model_width:]

    def own_part(array):
        return lax.dynamic_slice_in_dim(array, col_index * own_len, own_len, axis=0)

    residual = embedded.astype(f32)
    inverse_own = own_part(inverse)[:, None]
    layer_out = (residual + branch_sum).astype(bf16)
    grad_input = (
        out_grad.astype(f32)
        + inverse_own * (grad_normed * norm_gain[None, :])
        - residual * (inverse_own**2 * own_part(dot_sum)[:, None] / D)
    ).astype(bf16)
    return (layer_out, grad_input, grad_gain, grad_wq, grad_wk, grad_wv, grad_wo)


def solution(mesh):
    placed = (
        P("col"),
        P("col"),
        P(),
        P(None, ("row", "seq")),
        P(None, ("row", "seq")),
        P(("row", "seq")),
        P(("row", "seq"), "col"),
        P(("row", "seq"), "col"),
        P(("row", "seq"), "col"),
        P("col", ("row", "seq")),
        P("col", ("row", "seq")),
    )
    groups = mesh.shape["row"] * mesh.shape["seq"]
    heads_col = H // mesh.shape["col"]
    whole_heads = (
        heads_col == 2 * groups
        and KV // mesh.shape["col"] == mesh.shape["row"]
        and mesh.shape["seq"] == 4
    )
    return jax.shard_map(
        fast_device if whole_heads else general_device,
        mesh=mesh,
        in_specs=placed,
        out_specs=(
            P("col", ("row", "seq")),
            P("col", ("row", "seq")),
            P(("row", "seq")),
            P(("row", "seq"), "col"),
            P(("row", "seq"), "col"),
            P(("row", "seq"), "col"),
            P("col", ("row", "seq")),
        ),
        check_vma=False,
    )
```

```python
import jax
import jax.numpy as jnp
from jax import lax
from jax.experimental import pallas as pl
from jax.experimental.pallas import tpu as pltpu
from jax.sharding import PartitionSpec as P

D = 8192
H = 64
KV = 8
HD = 128


epsilon = 1e-05
softcap = 20.0
rope_base = 500000.0


def rotary_tables(positions, head_size):
    half_size = head_size // 2
    frequency = rope_base ** (-(jnp.arange(half_size, dtype=jnp.float32) * 2.0) / head_size)
    angles = positions.astype(jnp.float32)[:, None] * frequency[None, :]
    return (jnp.cos(angles), jnp.sin(angles))


def rotate_pairs(values, cosines, sines):
    half_size = values.shape[-1] // 2
    first_half = values[..., :half_size]
    second_half = values[..., half_size:]
    cos_part = cosines[:, None, :]
    sin_part = sines[:, None, :]
    return jnp.concatenate(
        [
            first_half * cos_part - second_half * sin_part,
            second_half * cos_part + first_half * sin_part,
        ],
        axis=-1,
    )


def rotate_back(values, cosines, sines):
    half_size = values.shape[-1] // 2
    first_half = values[..., :half_size]
    second_half = values[..., half_size:]
    cos_part = cosines[:, None, :]
    sin_part = sines[:, None, :]
    return jnp.concatenate(
        [
            first_half * cos_part + second_half * sin_part,
            second_half * cos_part - first_half * sin_part,
        ],
        axis=-1,
    )


def rope_round(values, positions):
    cosines, sines = rotary_tables(positions, HD)
    row_total = values.shape[0]
    return (
        rotate_pairs(values.reshape(row_total, -1, HD), cosines, sines)
        .reshape(row_total, -1)
        .astype(jnp.bfloat16)
    )


def plain_round(values, positions):
    return values.astype(jnp.bfloat16)


def general_device(
    motion_ids,
    audio_ids,
    segment_ids,
    motion_table,
    audio_table,
    norm_gain,
    w_query,
    w_key,
    w_value,
    w_out,
    out_grad,
):
    seq_len = segment_ids.shape[0]
    row_devices = lax.axis_size("row")
    seq_devices = lax.axis_size("seq")
    row_index = lax.axis_index("row")
    seq_index = lax.axis_index("seq")
    col_index = lax.axis_index("col")
    block_len = seq_len // (row_devices * seq_devices)
    quarter_len = seq_len // row_devices
    query_width = w_query.shape[1]
    kv_width = w_key.shape[1]
    heads_col = query_width // HD
    kv_col = kv_width // HD
    group_size = H // KV
    score_scale = HD ** (-0.5)
    block_pos = (row_index * seq_devices + seq_index) * block_len + jnp.arange(
        block_len, dtype=jnp.int32
    )
    embedded = (
        jnp.take(motion_table, motion_ids, axis=0).astype(jnp.float32)
        + jnp.take(audio_table, audio_ids, axis=0).astype(jnp.float32)
    ).astype(jnp.bfloat16)
    residual = embedded.astype(jnp.float32)
    squares = lax.psum(jnp.sum(residual * residual, axis=1), ("row", "seq"))
    inverse = lax.rsqrt(squares / D + epsilon)
    normed = (residual * inverse[:, None] * norm_gain[None, :]).astype(jnp.bfloat16)
    normed_all = lax.all_gather(normed, "col", axis=0, tiled=True)
    query_pos = row_index * quarter_len + jnp.arange(quarter_len, dtype=jnp.int32)
    head_first = col_index * heads_col + seq_index * (heads_col // seq_devices)
    head_count = heads_col // seq_devices

    def to_heads(term, finish):
        own_share = lax.psum_scatter(
            term(jnp.int32(0), block_len * lax.axis_size(("row", "seq"))),
            ("row", "seq"),
            scatter_dimension=0,
            tiled=True,
        )
        return lax.all_to_all(
            finish(own_share, block_pos), "seq", split_axis=1, concat_axis=0, tiled=True
        )

    def to_rows(heads_part):
        own_share = lax.all_to_all(heads_part, "seq", split_axis=0, concat_axis=1, tiled=True)
        return lax.all_gather(own_share, ("row", "seq"), axis=0, tiled=True)

    def query_term(first_row, row_count):
        return jnp.dot(normed_all, w_query, preferred_element_type=jnp.float32)

    queries = to_heads(query_term, rope_round)
    picked = normed_all
    kv_sum = lax.psum_scatter(
        jnp.concatenate(
            [
                jnp.dot(picked, w_key, preferred_element_type=jnp.float32),
                jnp.dot(picked, w_value, preferred_element_type=jnp.float32),
            ],
            axis=1,
        ),
        ("row", "seq"),
        scatter_dimension=0,
        tiled=True,
    )
    kv_block = jnp.concatenate(
        [rope_round(kv_sum[:, :kv_width], block_pos), kv_sum[:, kv_width:].astype(jnp.bfloat16)],
        axis=1,
    )
    kv_all = lax.all_gather(kv_block, ("row", "seq"), axis=0, tiled=True)
    query_len = queries.shape[0]
    kv_slot = (
        head_first + jnp.arange(head_count, dtype=jnp.int32)
    ) // group_size - col_index * kv_col
    key_sel = jnp.take(kv_all[:, :kv_width].reshape(seq_len, kv_col, HD), kv_slot, axis=1)
    value_sel = jnp.take(kv_all[:, kv_width:].reshape(seq_len, kv_col, HD), kv_slot, axis=1)
    key_pos = jnp.arange(seq_len, dtype=jnp.int32)
    allowed = (key_pos[None, :] <= query_pos[:, None]) & (
        segment_ids[None, :] == jnp.take(segment_ids, query_pos)[:, None]
    )
    query_heads = queries.reshape(query_len, head_count, HD)
    raw_scores = (
        jnp.einsum("qhd,khd->hqk", query_heads, key_sel, preferred_element_type=jnp.float32)
        * score_scale
    )
    capped = softcap * jnp.tanh(raw_scores / softcap)
    weights = jnp.where(allowed[None], jnp.exp(capped), 0.0)
    totals = jnp.sum(weights, axis=2)
    attended = jnp.einsum(
        "hqk,khd->qhd", weights.astype(jnp.bfloat16), value_sel, preferred_element_type=jnp.float32
    )
    attn_out = (
        (attended / totals.T[:, :, None]).astype(jnp.bfloat16).reshape(query_len, head_count * HD)
    )
    out_all = to_rows(attn_out)
    picked = out_all
    branch_sum = lax.psum_scatter(
        jnp.dot(picked, w_out, preferred_element_type=jnp.float32).astype(jnp.bfloat16),
        "col",
        scatter_dimension=0,
        tiled=True,
    ).astype(jnp.float32)
    layer_out = (residual + branch_sum).astype(jnp.bfloat16)
    grad_all = lax.all_gather(out_grad, "col", axis=0, tiled=True)
    grad_wo = jnp.einsum("ln,ld->nd", out_all, grad_all, preferred_element_type=jnp.float32)

    def dout_term(first_row, row_count):
        return jnp.einsum("ld,nd->ln", grad_all, w_out, preferred_element_type=jnp.float32)

    out_heads = to_heads(dout_term, plain_round).reshape(query_len, head_count, HD)
    attn_probs = weights / totals[:, :, None]
    prob_grads = jnp.einsum(
        "qhd,khd->hqk", out_heads, value_sel, preferred_element_type=jnp.float32
    )
    row_dots = jnp.sum(attn_probs * prob_grads, axis=2, keepdims=True)
    grad_scores = (
        attn_probs * (prob_grads - row_dots) * (1.0 - (capped / softcap) ** 2) * score_scale
    ).astype(jnp.bfloat16)
    grad_query = jnp.einsum(
        "hqk,khd->qhd", grad_scores, key_sel, preferred_element_type=jnp.float32
    )
    grad_key_heads = jnp.einsum(
        "hqk,qhd->khd", grad_scores, query_heads, preferred_element_type=jnp.float32
    )
    grad_value_heads = jnp.einsum(
        "hqk,qhd->khd",
        attn_probs.astype(jnp.bfloat16),
        out_heads,
        preferred_element_type=jnp.float32,
    )
    slot_mask = (kv_slot[:, None] == jnp.arange(kv_col, dtype=jnp.int32)[None, :]).astype(
        jnp.float32
    )
    grad_key_part = jnp.sum(
        grad_key_heads[:, :, None, :] * slot_mask[None, :, :, None], axis=1
    ).reshape(seq_len, kv_width)
    grad_value_part = jnp.sum(
        grad_value_heads[:, :, None, :] * slot_mask[None, :, :, None], axis=1
    ).reshape(seq_len, kv_width)
    kv_grad_sum = lax.psum_scatter(
        jnp.concatenate([grad_key_part, grad_value_part], axis=1).astype(jnp.bfloat16),
        ("row", "seq"),
        scatter_dimension=0,
        tiled=True,
    ).astype(jnp.float32)
    cos_block, sin_block = rotary_tables(block_pos, HD)
    grad_key_block = (
        rotate_back(kv_grad_sum[:, :kv_width].reshape(block_len, kv_col, HD), cos_block, sin_block)
        .reshape(block_len, kv_width)
        .astype(jnp.bfloat16)
    )
    kv_grad_block = jnp.concatenate(
        [grad_key_block, kv_grad_sum[:, kv_width:].astype(jnp.bfloat16)], axis=1
    )
    kv_grad_all = lax.all_gather(kv_grad_block, ("row", "seq"), axis=0, tiled=True)
    cos_query, sin_query = rotary_tables(query_pos, HD)
    grad_query_round = (
        rotate_back(grad_query, cos_query, sin_query)
        .reshape(query_len, head_count * HD)
        .astype(jnp.bfloat16)
    )
    grad_query_all = to_rows(grad_query_round)
    grad_wq = jnp.einsum(
        "ld,ln->dn", normed_all, grad_query_all, preferred_element_type=jnp.float32
    )
    grad_wk = jnp.einsum(
        "ld,ln->dn", normed_all, kv_grad_all[:, :kv_width], preferred_element_type=jnp.float32
    )
    grad_wv = jnp.einsum(
        "ld,ln->dn", normed_all, kv_grad_all[:, kv_width:], preferred_element_type=jnp.float32
    )
    total_term = jnp.einsum(
        "ln,dn->ld", grad_query_all, w_query, preferred_element_type=jnp.float32
    )
    total_term = total_term + jnp.einsum(
        "ln,dn->ld", kv_grad_all[:, :kv_width], w_key, preferred_element_type=jnp.float32
    )
    grad_normed = lax.psum_scatter(
        (
            total_term
            + jnp.einsum(
                "ln,dn->ld", kv_grad_all[:, kv_width:], w_value, preferred_element_type=jnp.float32
            )
        ).astype(jnp.bfloat16),
        "col",
        scatter_dimension=0,
        tiled=True,
    ).astype(jnp.float32)
    scaled_grad = grad_normed * norm_gain[None, :]
    total_dot = lax.psum(jnp.sum(scaled_grad * residual, axis=1), ("row", "seq"))
    grad_input = (
        out_grad.astype(jnp.float32)
        + inverse[:, None] * scaled_grad
        - residual * (inverse**3 * total_dot / D)[:, None]
    ).astype(jnp.bfloat16)
    grad_gain = lax.psum(jnp.sum(grad_normed * residual * inverse[:, None], axis=0), "col")
    return (layer_out, grad_input, grad_gain, grad_wq, grad_wk, grad_wv, grad_wo)


VMEM_BYTES = 56 * 1024 * 1024


def remote(source, target, send_sem, recv_sem, place):
    copy = pltpu.make_async_remote_copy(
        src_ref=source,
        dst_ref=target,
        send_sem=send_sem,
        recv_sem=recv_sem,
        device_id=place,
        device_id_type=pl.DeviceIdType.MESH,
    )
    copy.start()
    return copy


def greet(places):
    barrier = pltpu.get_barrier_semaphore()
    for place in places:
        pl.semaphore_signal(
            barrier, inc=1, device_id=place, device_id_type=pl.DeviceIdType.MESH
        )
    pl.semaphore_wait(barrier, len(places))


def neighbours():
    row = lax.axis_index("row")
    seq = lax.axis_index("seq")
    rows = lax.axis_size("row")
    across, core = seq // 2, seq % 2
    plane = [(across, 1 - core), (1 - across, core), (1 - across, 1 - core)]
    plane_ids = [{"row": row, "seq": 2 * a + c} for a, c in plane]
    plane_slots = [2 * c + a for a, c in plane]
    others = [(row + step) % rows for step in range(1, rows)]
    row_ids = [{"row": other, "seq": seq} for other in others]
    return row, across, core, plane_ids, plane_slots, others, row_ids


def reduce_kernel(
    q_part, o_part, kv_part, sq_part,
    q_out, o_out, kv_out, sq_out,
    q_rc, o_rc, kv_rc, q_a1, o_a1, kv_a1, q_rx, o_rx, kv_rx, q_a2, o_a2, kv_a2,
    q_rz, o_rz, kv_rz, kv_own, kv_all, sq_send, sq_recv,
    core_send, core_recv, x_send, x_recv, z_send, z_recv, kv_send, kv_recv, sq_ss, sq_rs,
):
    f32, bf16 = jnp.float32, jnp.bfloat16
    row, across, core, plane_ids, plane_slots, others, row_ids = neighbours()
    rows = len(others) + 1
    core_id, x_id = plane_ids[0], plane_ids[1]
    greet(plane_ids + row_ids)
    seq_len = q_out.shape[0]
    width = q_out.shape[1]
    block = seq_len // 4
    wide = 2 * width
    half_len = seq_len // 2
    pieces = [(None, 0)] + [(0, b) for b in range(4)] + [(1, b) for b in range(4)]
    parts, rcs, a1s = (q_part, o_part), (q_rc, o_rc), (q_a1, o_a1)
    rxs, a2s, rzs, outs = (q_rx, o_rx), (q_a2, o_a2), (q_rz, o_rz), (q_out, o_out)
    core_copies, x_copies, z_copies = [], [], []

    sq_copy = remote(sq_part, sq_recv.at[0], sq_ss.at[0], sq_rs.at[0], core_id)

    def start_core(index):
        which, b = pieces[index]
        copies = []
        if which is None:
            source = kv_part.at[pl.ds(pl.multiple_of((1 - core) * half_len, half_len), half_len)]
            copies.append(
                remote(source, kv_rc, core_send.at[index, 0], core_recv.at[index, 0], core_id)
            )
        else:
            lines = pl.ds(b * block, block)
            for r in range(rows):
                first = pl.multiple_of(r * 2 * wide + (1 - core) * wide, wide)
                copies.append(
                    remote(
                        parts[which].at[lines, pl.ds(first, wide)],
                        rcs[which].at[lines, pl.ds(r * wide, wide)],
                        core_send.at[index, r],
                        core_recv.at[index, r],
                        core_id,
                    )
                )
        core_copies.append(copies)

    for index in range(3):
        start_core(index)

    def core_stage(index):
        which, b = pieces[index]
        for copy in core_copies[index]:
            copy.wait_recv()
        if index + 3 < len(pieces):
            start_core(index + 3)
        if which is None:
            own = kv_part[pl.ds(pl.multiple_of(core * half_len, half_len), half_len), :]
            kv_a1[...] = (own.astype(f32) + kv_rc[...].astype(f32)).astype(bf16)
            source = kv_a1.at[pl.ds(pl.multiple_of((1 - across) * block, block), block)]
            target = kv_rx
        else:
            lines = pl.ds(b * block, block)
            for r in range(rows):
                for side in range(2):
                    first = pl.multiple_of(r * 2 * wide + core * wide + side * width, width)
                    total = parts[which][lines, pl.ds(first, width)].astype(f32) + rcs[which][
                        lines, pl.ds(r * wide + side * width, width)
                    ].astype(f32)
                    a1s[which][side, lines, pl.ds(r * width, width)] = total.astype(bf16)
            source = a1s[which].at[1 - across, lines]
            target = rxs[which].at[lines]
        x_copies.append(remote(source, target, x_send.at[index], x_recv.at[index], x_id))

    def x_stage(index):
        which, b = pieces[index]
        x_copies[index].wait_recv()
        lines = pl.ds(b * block, block)
        if which is None:
            held = kv_a1[pl.ds(pl.multiple_of(across * block, block), block), :]
            got, kept, landing, span = kv_rx[...], kv_a2, kv_rz, pl.ds(0, block)
        else:
            held = a1s[which][across, lines, :]
            got, kept, landing, span = rxs[which][lines, :], a2s[which], rzs[which], lines
        total = (held.astype(f32) + got.astype(f32)).astype(bf16)
        for r in range(rows):
            kept[r, span, :] = total[:, r * width : (r + 1) * width]
        z_copies.append(
            [
                remote(
                    kept.at[others[step], span],
                    landing.at[step, span],
                    z_send.at[index, step],
                    z_recv.at[index, step],
                    row_ids[step],
                )
                for step in range(rows - 1)
            ]
        )

    def z_stage(index):
        which, b = pieces[index]
        for copy in z_copies[index]:
            copy.wait_recv()
        lines = pl.ds(b * block, block)
        if which is None:
            kept, landing, span = kv_a2, kv_rz, pl.ds(0, block)
        else:
            kept, landing, span = a2s[which], rzs[which], lines
        total = kept[row, span, :].astype(f32)
        for step in range(rows - 1):
            total = total + landing[step, span, :].astype(f32)
        if which is None:
            kv_own[...] = total
            return [
                remote(
                    kv_own, kv_all.at[step], kv_send.at[step], kv_recv.at[step], plane_ids[step]
                )
                for step in range(3)
            ]
        outs[which][lines, :] = total.astype(outs[which].dtype)
        return []

    kv_copies = []
    sq_copies = [sq_copy]
    for turn in range(len(pieces) + 5):
        if turn < len(pieces):
            core_stage(turn)
        if turn == 1:
            sq_copies[0].wait_recv()
            sq_send[0] = sq_part[...] + sq_recv[0]
            sq_copies.append(
                remote(sq_send.at[0], sq_recv.at[1], sq_ss.at[1], sq_rs.at[1], x_id)
            )
        if turn == 3:
            sq_copies[1].wait_recv()
            sq_send[1] = sq_send[0] + sq_recv[1]
            for step in range(rows - 1):
                sq_copies.append(
                    remote(
                        sq_send.at[1],
                        sq_recv.at[2 + step],
                        sq_ss.at[2 + step],
                        sq_rs.at[2 + step],
                        row_ids[step],
                    )
                )
        if 2 <= turn <= len(pieces) + 1:
            x_stage(turn - 2)
        if turn >= 5:
            kv_copies += z_stage(turn - 5)
    total = sq_send[1]
    for step in range(rows - 1):
        sq_copies[2 + step].wait_recv()
        total = total + sq_recv[2 + step]
    sq_out[...] = total
    own_slot = 2 * core + across
    kv_out[pl.ds(pl.multiple_of(own_slot * block, block), block), :] = kv_own[...]
    for step in range(3):
        kv_copies[step].wait_recv()
        first = pl.multiple_of(plane_slots[step] * block, block)
        kv_out[pl.ds(first, block), :] = kv_all[step]
    for copy in sum(core_copies, []) + x_copies + sum(z_copies, []) + kv_copies + sq_copies:
        copy.wait_send()


def reduce_shares(q_part, o_part, kv_part, sq_part, rows):
    f32, bf16 = jnp.float32, jnp.bfloat16
    seq_len, whole = q_part.shape
    width = whole // (4 * rows)
    block = seq_len // 4
    dma = pltpu.SemaphoreType.DMA
    twice = lambda *shape: [pltpu.VMEM(shape, bf16)] * 2
    return pl.pallas_call(
        reduce_kernel,
        out_shape=(
            jax.ShapeDtypeStruct((seq_len, width), f32),
            jax.ShapeDtypeStruct((seq_len, width), bf16),
            jax.ShapeDtypeStruct((seq_len, width), f32),
            jax.ShapeDtypeStruct(sq_part.shape, f32),
        ),
        in_specs=[pl.BlockSpec(memory_space=pltpu.VMEM)] * 4,
        out_specs=[pl.BlockSpec(memory_space=pltpu.VMEM)] * 4,
        scratch_shapes=[
            *twice(seq_len, whole // 2),
            pltpu.VMEM((seq_len // 2, rows * width), bf16),
            *twice(2, seq_len, rows * width),
            pltpu.VMEM((seq_len // 2, rows * width), bf16),
            *twice(seq_len, rows * width),
            pltpu.VMEM((block, rows * width), bf16),
            *twice(rows, seq_len, width),
            pltpu.VMEM((rows, block, width), bf16),
            *twice(rows - 1, seq_len, width),
            pltpu.VMEM((rows - 1, block, width), bf16),
            pltpu.VMEM((block, width), f32),
            pltpu.VMEM((3, block, width), f32),
            pltpu.VMEM((2, *sq_part.shape), f32),
            pltpu.VMEM((1 + rows, *sq_part.shape), f32),
            dma((9, rows)), dma((9, rows)), dma((9,)), dma((9,)),
            dma((9, rows - 1)), dma((9, rows - 1)), dma((3,)), dma((3,)),
            dma((1 + rows,)), dma((1 + rows,)),
        ],
        compiler_params=pltpu.CompilerParams(
            collective_id=0, has_side_effects=True, vmem_limit_bytes=VMEM_BYTES
        ),
    )(q_part, o_part, kv_part, sq_part)


def gather_kernel(
    q_sum, o_heads, kv_sum, squares, mask, cos_ref, sin_ref,
    a_all, q_all, kv_all, dot_out,
    a_own, q_own, kv_part, q_heads, probs, tanhs, dot_part,
    kv_recv_buf, dot_send, dot_recv,
    z_send, z_recv, x_send, x_recv, core_send, core_recv,
    r_send, r_recv, kz_send, kz_recv, kp_send, kp_recv, dot_ss, dot_rs,
):
    f32, bf16 = jnp.float32, jnp.bfloat16
    row, across, core, plane_ids, plane_slots, others, row_ids = neighbours()
    rows = len(others) + 1
    core_id, x_id = plane_ids[0], plane_ids[1]
    seq_len, width = a_own.shape
    block = seq_len // 4
    wide = 2 * width
    head = width // 2
    own_slot = 2 * core + across
    own_first = pl.multiple_of(row * 2 * wide + own_slot * width, width)
    own_lines = pl.ds(pl.multiple_of(own_slot * block, block), block)
    own_kv = pl.ds(pl.multiple_of(row * width, width), width)
    greet(plane_ids + row_ids)

    def swapped(values):
        return jnp.concatenate([values[:, head // 2 :], values[:, : head // 2]], axis=1)

    def dot(left, right, dims):
        return lax.dot_general(left, right, ((dims[:1], dims[1:]), ((), ())), preferred_element_type=f32)

    score_scale = HD ** (-0.5)
    inverse = jnp.broadcast_to(lax.rsqrt(squares[0:1, :] / D + epsilon), (head, seq_len)).T
    key_raw = kv_sum[:, :head] * inverse
    keys = (key_raw * cos_ref[...] + swapped(key_raw) * sin_ref[...]).astype(bf16)
    values = (kv_sum[:, head:] * inverse).astype(bf16)
    for h in range(2):
        lanes = pl.ds(h * head, head)
        raw = q_sum[:, lanes] * inverse
        query = (raw * cos_ref[...] + swapped(raw) * sin_ref[...]).astype(bf16)
        q_heads[:, lanes] = query
        tanh_scores = jnp.tanh(dot(query, keys, (1, 1)) * (score_scale / softcap))
        weights = jnp.exp(softcap * tanh_scores) * mask[...]
        totals = jnp.sum(weights, axis=1, keepdims=True)
        attended = dot(weights.astype(bf16), values, (1, 0))
        a_own[:, lanes] = (attended / totals).astype(bf16)
        probs[h] = weights / totals
        tanhs[h] = tanh_scores

    pieces = [(which, b) for which in range(2) for b in range(4)]
    owns, alls = (a_own, q_own), (a_all, q_all)
    z_copies, x_copies, core_copies = [], [], []

    def start_z(index):
        which, b = pieces[index]
        lines = pl.ds(b * block, block)
        z_copies.append(
            [
                remote(
                    owns[which].at[lines],
                    alls[which].at[lines, pl.ds(own_first, width)],
                    z_send.at[index, step],
                    z_recv.at[index, step],
                    row_ids[step],
                )
                for step in range(rows - 1)
            ]
        )

    for index in range(3):
        start_z(index)
    a_all[:, pl.ds(own_first, width)] = a_own[...]

    dots = jnp.zeros((seq_len, head), f32)
    grad_key = jnp.zeros((seq_len, head), f32)
    grad_value = jnp.zeros((seq_len, head), f32)
    for h in range(2):
        lanes = pl.ds(h * head, head)
        out_head, query, prob = o_heads[:, lanes], q_heads[:, lanes], probs[h]
        prob_grads = dot(out_head, values, (1, 1))
        row_dots = jnp.sum(prob * prob_grads, axis=1, keepdims=True)
        grad_scores = (
            prob * (prob_grads - row_dots) * (1.0 - tanhs[h] * tanhs[h]) * score_scale
        ).astype(bf16)
        grad_query = dot(grad_scores, keys, (1, 0))
        grad_key = grad_key + dot(grad_scores, query, (0, 0))
        grad_value = grad_value + dot(prob.astype(bf16), out_head, (0, 0))
        dots = dots + grad_query * query.astype(f32)
        q_own[:, lanes] = (
            grad_query * cos_ref[...] - swapped(grad_query) * sin_ref[...]
        ).astype(bf16)
    dots = dots + grad_key * keys.astype(f32) + grad_value * values.astype(f32)
    dot_part[...] = jnp.broadcast_to(jnp.sum(dots.T, axis=0, keepdims=True), dot_part.shape)
    kv_part[:, :head] = grad_key.astype(bf16)
    kv_part[:, head:] = grad_value.astype(bf16)
    q_all[:, pl.ds(own_first, width)] = q_own[...]

    reduces = []
    for step in range(3):
        first = pl.multiple_of(plane_slots[step] * block, block)
        reduces.append(
            remote(
                kv_part.at[pl.ds(first, block)],
                kv_recv_buf.at[step],
                r_send.at[step],
                r_recv.at[step],
                plane_ids[step],
            )
        )
    dot_copies = [
        remote(dot_part, dot_recv.at[step], dot_ss.at[step], dot_rs.at[step], row_ids[step])
        for step in range(rows - 1)
    ]
    def finish_kv():
        total = kv_part[own_lines, :].astype(f32)
        for step in range(3):
            reduces[step].wait_recv()
            total = total + kv_recv_buf[step].astype(f32)
        key_part = total[:, :head]
        key_part = key_part * cos_ref[own_lines, :] - swapped(key_part) * sin_ref[own_lines, :]
        kv_all[own_lines, own_kv] = jnp.concatenate([key_part, total[:, head:]], axis=1).astype(
            bf16
        )
        return [
            remote(
                kv_all.at[own_lines, own_kv],
                kv_all.at[own_lines, own_kv],
                kz_send.at[step],
                kz_recv.at[step],
                row_ids[step],
            )
            for step in range(rows - 1)
        ]

    def x_stage(index):
        which, b = pieces[index]
        lines = pl.ds(b * block, block)
        for copy in z_copies[index]:
            copy.wait_recv()
        if index + 3 < len(pieces):
            start_z(index + 3)
        copies = []
        for r in range(rows):
            first = pl.multiple_of(r * 2 * wide + own_slot * width, width)
            place = alls[which].at[lines, pl.ds(first, width)]
            copies.append(remote(place, place, x_send.at[index, r], x_recv.at[index, r], x_id))
        x_copies.append(copies)

    def core_stage(index):
        which, b = pieces[index]
        lines = pl.ds(b * block, block)
        for copy in x_copies[index]:
            copy.wait_recv()
        copies = []
        for r in range(rows):
            first = pl.multiple_of(r * 2 * wide + core * wide, wide)
            place = alls[which].at[lines, pl.ds(first, wide)]
            copies.append(
                remote(place, place, core_send.at[index, r], core_recv.at[index, r], core_id)
            )
        core_copies.append(copies)

    kv_plane = []
    for turn in range(len(pieces) + 2):
        if turn < len(pieces):
            x_stage(turn)
        if turn == 0:
            total = dot_part[...]
            for step in range(rows - 1):
                dot_copies[step].wait_recv()
                total = total + dot_recv[step]
            dot_send[0] = total
            dot_copies.append(
                remote(
                    dot_send.at[0],
                    dot_recv.at[rows - 1],
                    dot_ss.at[rows - 1],
                    dot_rs.at[rows - 1],
                    x_id,
                )
            )
        if turn == 1:
            kv_z = finish_kv()
        if turn == 4:
            for copy in kv_z:
                copy.wait_recv()
            kv_plane = [
                remote(
                    kv_all.at[own_lines],
                    kv_all.at[own_lines],
                    kp_send.at[step],
                    kp_recv.at[step],
                    plane_ids[step],
                )
                for step in range(3)
            ]
        if turn == 2:
            dot_copies[rows - 1].wait_recv()
            dot_send[1] = dot_send[0] + dot_recv[rows - 1]
            dot_copies.append(
                remote(
                    dot_send.at[1], dot_recv.at[rows], dot_ss.at[rows], dot_rs.at[rows], core_id
                )
            )
        if turn >= 2:
            core_stage(turn - 2)
    dot_copies[rows].wait_recv()
    dot_out[...] = dot_send[1] + dot_recv[rows]
    for copy in kv_plane + sum(core_copies, []):
        copy.wait_recv()
    for copy in (
        sum(z_copies + x_copies + core_copies, []) + reduces + kv_z + kv_plane + dot_copies
    ):
        copy.wait_send()


def attend_and_gather(q_sum, o_heads, kv_sum, squares, mask, cosines, sines, rows):
    f32, bf16 = jnp.float32, jnp.bfloat16
    seq_len, width = q_sum.shape
    block = seq_len // 4
    whole = width * 4 * rows
    dma = pltpu.SemaphoreType.DMA
    return pl.pallas_call(
        gather_kernel,
        out_shape=(
            jax.ShapeDtypeStruct((seq_len, whole), bf16),
            jax.ShapeDtypeStruct((seq_len, whole), bf16),
            jax.ShapeDtypeStruct((seq_len, rows * width), bf16),
            jax.ShapeDtypeStruct(squares.shape, f32),
        ),
        in_specs=[pl.BlockSpec(memory_space=pltpu.VMEM)] * 7,
        out_specs=[pl.BlockSpec(memory_space=pltpu.VMEM)] * 4,
        scratch_shapes=[
            *[pltpu.VMEM((seq_len, width), bf16)] * 4,
            *[pltpu.VMEM((2, seq_len, seq_len), f32)] * 2,
            pltpu.VMEM(squares.shape, f32),
            pltpu.VMEM((3, block, width), bf16),
            pltpu.VMEM((2, *squares.shape), f32),
            pltpu.VMEM((rows + 1, *squares.shape), f32),
            dma((8, rows - 1)), dma((8, rows - 1)), dma((8, rows)), dma((8, rows)),
            dma((8, rows)), dma((8, rows)), dma((3,)), dma((3,)),
            dma((rows - 1,)), dma((rows - 1,)), dma((3,)), dma((3,)),
            dma((rows + 1,)), dma((rows + 1,)),
        ],
        compiler_params=pltpu.CompilerParams(
            collective_id=1, has_side_effects=True, vmem_limit_bytes=VMEM_BYTES
        ),
    )(q_sum, o_heads, kv_sum, squares, mask, cosines, sines)


def fast_device(
    motion_ids,
    audio_ids,
    segment_ids,
    motion_table,
    audio_table,
    norm_gain,
    w_query,
    w_key,
    w_value,
    w_out,
    out_grad,
):
    f32, bf16 = jnp.float32, jnp.bfloat16
    seq_len = segment_ids.shape[0]
    row_devices = lax.axis_size("row")
    col_index = lax.axis_index("col")
    own_len = out_grad.shape[0]
    model_width = out_grad.shape[1]
    kv_width = w_key.shape[1]

    embedded = (
        motion_table.at[motion_ids].get(mode="promise_in_bounds").astype(f32)
        + audio_table.at[audio_ids].get(mode="promise_in_bounds").astype(f32)
    ).astype(bf16)
    both = lax.all_gather(
        jnp.concatenate([embedded, out_grad], axis=1), "col", axis=0, tiled=True
    )
    embedded_all = both[:, :model_width]
    grad_all = both[:, model_width:]
    residual_all = embedded_all.astype(f32)
    scaled = (residual_all * norm_gain[None, :]).astype(bf16)

    def product(left, right):
        return jnp.dot(left, right, preferred_element_type=f32).astype(bf16)

    def as_rows(vector):
        return jnp.broadcast_to(vector[None, :], (8, seq_len))

    kv_part = jnp.concatenate(
        [
            product(scaled, w_key).reshape(seq_len, row_devices, HD),
            product(scaled, w_value).reshape(seq_len, row_devices, HD),
        ],
        axis=2,
    ).reshape(seq_len, 2 * kv_width)
    out_part = jnp.einsum("ld,nd->ln", grad_all, w_out, preferred_element_type=f32).astype(bf16)
    query_sum, out_heads, kv_sum, squares = reduce_shares(
        product(scaled, w_query),
        out_part,
        kv_part,
        as_rows(jnp.sum(residual_all * residual_all, axis=1)),
        row_devices,
    )
    inverse = lax.rsqrt(squares[0] / D + epsilon)
    positions = jnp.arange(seq_len, dtype=jnp.int32)
    cosines, sines = rotary_tables(positions, HD)
    allowed = (positions[None, :] <= positions[:, None]) & (
        segment_ids[None, :] == segment_ids[:, None]
    )
    out_all, grad_query_all, kv_grad_all, dot_sum = attend_and_gather(
        query_sum,
        out_heads,
        kv_sum,
        squares,
        allowed.astype(f32),
        jnp.concatenate([cosines, cosines], axis=1),
        jnp.concatenate([-sines, sines], axis=1),
        row_devices,
    )
    kv_grad_all = kv_grad_all.reshape(seq_len, row_devices, 2 * HD)
    grad_key_all = kv_grad_all[:, :, :HD].reshape(seq_len, kv_width)
    grad_value_all = kv_grad_all[:, :, HD:].reshape(seq_len, kv_width)

    normed = (residual_all * inverse[:, None] * norm_gain[None, :]).astype(bf16)
    branch_part = product(out_all, w_out)
    grad_wo = jnp.einsum("ln,ld->nd", out_all, grad_all, preferred_element_type=f32)
    grad_wq = jnp.einsum("ld,ln->dn", normed, grad_query_all, preferred_element_type=f32)
    grad_wk = jnp.einsum("ld,ln->dn", normed, grad_key_all, preferred_element_type=f32)
    grad_wv = jnp.einsum("ld,ln->dn", normed, grad_value_all, preferred_element_type=f32)
    normed_part = (
        jnp.einsum("ln,dn->ld", grad_query_all, w_query, preferred_element_type=f32)
        + jnp.einsum("ln,dn->ld", grad_key_all, w_key, preferred_element_type=f32)
        + jnp.einsum("ln,dn->ld", grad_value_all, w_value, preferred_element_type=f32)
    )
    gain_part = jnp.sum(normed_part * residual_all * inverse[:, None], axis=0)
    branch_sum, grad_normed = (
        lax.psum_scatter(
            jnp.concatenate([branch_part, normed_part.astype(bf16)], axis=1),
            "col",
            scatter_dimension=0,
            tiled=True,
        )
        .astype(f32)
        .reshape(own_len, 2, model_width)
        .swapaxes(0, 1)
    )
    sums = lax.psum(jnp.concatenate([gain_part, dot_sum[0]]), "col")
    grad_gain, dot_sum = sums[:model_width], sums[model_width:]

    def own_part(array):
        return lax.dynamic_slice_in_dim(array, col_index * own_len, own_len, axis=0)

    residual = embedded.astype(f32)
    inverse_own = own_part(inverse)[:, None]
    layer_out = (residual + branch_sum).astype(bf16)
    grad_input = (
        out_grad.astype(f32)
        + inverse_own * (grad_normed * norm_gain[None, :])
        - residual * (inverse_own**2 * own_part(dot_sum)[:, None] / D)
    ).astype(bf16)
    return (layer_out, grad_input, grad_gain, grad_wq, grad_wk, grad_wv, grad_wo)


def solution(mesh):
    placed = (
        P("col"),
        P("col"),
        P(),
        P(None, ("row", "seq")),
        P(None, ("row", "seq")),
        P(("row", "seq")),
        P(("row", "seq"), "col"),
        P(("row", "seq"), "col"),
        P(("row", "seq"), "col"),
        P("col", ("row", "seq")),
        P("col", ("row", "seq")),
    )
    groups = mesh.shape["row"] * mesh.shape["seq"]
    heads_col = H // mesh.shape["col"]
    whole_heads = (
        heads_col == 2 * groups
        and KV // mesh.shape["col"] == mesh.shape["row"]
        and mesh.shape["seq"] == 4
    )
    return jax.shard_map(
        fast_device if whole_heads else general_device,
        mesh=mesh,
        in_specs=placed,
        out_specs=(
            P("col", ("row", "seq")),
            P("col", ("row", "seq")),
            P(("row", "seq")),
            P(("row", "seq"), "col"),
            P(("row", "seq"), "col"),
            P(("row", "seq"), "col"),
            P("col", ("row", "seq")),
        ),
        check_vma=False,
    )
```

```python
import jax
import jax.numpy as jnp
from jax import lax
from jax.experimental import pallas as pl
from jax.experimental.pallas import tpu as pltpu
from jax.sharding import PartitionSpec as P

D = 8192
H = 64
KV = 8
HD = 128


epsilon = 1e-05
softcap = 20.0
rope_base = 500000.0


def rotary_tables(positions, head_size):
    half_size = head_size // 2
    frequency = rope_base ** (-(jnp.arange(half_size, dtype=jnp.float32) * 2.0) / head_size)
    angles = positions.astype(jnp.float32)[:, None] * frequency[None, :]
    return (jnp.cos(angles), jnp.sin(angles))


def rotate_pairs(values, cosines, sines):
    half_size = values.shape[-1] // 2
    first_half = values[..., :half_size]
    second_half = values[..., half_size:]
    cos_part = cosines[:, None, :]
    sin_part = sines[:, None, :]
    return jnp.concatenate(
        [
            first_half * cos_part - second_half * sin_part,
            second_half * cos_part + first_half * sin_part,
        ],
        axis=-1,
    )


def rotate_back(values, cosines, sines):
    half_size = values.shape[-1] // 2
    first_half = values[..., :half_size]
    second_half = values[..., half_size:]
    cos_part = cosines[:, None, :]
    sin_part = sines[:, None, :]
    return jnp.concatenate(
        [
            first_half * cos_part + second_half * sin_part,
            second_half * cos_part - first_half * sin_part,
        ],
        axis=-1,
    )


def rope_round(values, positions):
    cosines, sines = rotary_tables(positions, HD)
    row_total = values.shape[0]
    return (
        rotate_pairs(values.reshape(row_total, -1, HD), cosines, sines)
        .reshape(row_total, -1)
        .astype(jnp.bfloat16)
    )


def plain_round(values, positions):
    return values.astype(jnp.bfloat16)


def general_device(
    motion_ids,
    audio_ids,
    segment_ids,
    motion_table,
    audio_table,
    norm_gain,
    w_query,
    w_key,
    w_value,
    w_out,
    out_grad,
):
    seq_len = segment_ids.shape[0]
    row_devices = lax.axis_size("row")
    seq_devices = lax.axis_size("seq")
    row_index = lax.axis_index("row")
    seq_index = lax.axis_index("seq")
    col_index = lax.axis_index("col")
    block_len = seq_len // (row_devices * seq_devices)
    quarter_len = seq_len // row_devices
    query_width = w_query.shape[1]
    kv_width = w_key.shape[1]
    heads_col = query_width // HD
    kv_col = kv_width // HD
    group_size = H // KV
    score_scale = HD ** (-0.5)
    block_pos = (row_index * seq_devices + seq_index) * block_len + jnp.arange(
        block_len, dtype=jnp.int32
    )
    embedded = (
        jnp.take(motion_table, motion_ids, axis=0).astype(jnp.float32)
        + jnp.take(audio_table, audio_ids, axis=0).astype(jnp.float32)
    ).astype(jnp.bfloat16)
    residual = embedded.astype(jnp.float32)
    squares = lax.psum(jnp.sum(residual * residual, axis=1), ("row", "seq"))
    inverse = lax.rsqrt(squares / D + epsilon)
    normed = (residual * inverse[:, None] * norm_gain[None, :]).astype(jnp.bfloat16)
    normed_all = lax.all_gather(normed, "col", axis=0, tiled=True)
    query_pos = row_index * quarter_len + jnp.arange(quarter_len, dtype=jnp.int32)
    head_first = col_index * heads_col + seq_index * (heads_col // seq_devices)
    head_count = heads_col // seq_devices

    def to_heads(term, finish):
        own_share = lax.psum_scatter(
            term(jnp.int32(0), block_len * lax.axis_size(("row", "seq"))),
            ("row", "seq"),
            scatter_dimension=0,
            tiled=True,
        )
        return lax.all_to_all(
            finish(own_share, block_pos), "seq", split_axis=1, concat_axis=0, tiled=True
        )

    def to_rows(heads_part):
        own_share = lax.all_to_all(heads_part, "seq", split_axis=0, concat_axis=1, tiled=True)
        return lax.all_gather(own_share, ("row", "seq"), axis=0, tiled=True)

    def query_term(first_row, row_count):
        return jnp.dot(normed_all, w_query, preferred_element_type=jnp.float32)

    queries = to_heads(query_term, rope_round)
    picked = normed_all
    kv_sum = lax.psum_scatter(
        jnp.concatenate(
            [
                jnp.dot(picked, w_key, preferred_element_type=jnp.float32),
                jnp.dot(picked, w_value, preferred_element_type=jnp.float32),
            ],
            axis=1,
        ),
        ("row", "seq"),
        scatter_dimension=0,
        tiled=True,
    )
    kv_block = jnp.concatenate(
        [rope_round(kv_sum[:, :kv_width], block_pos), kv_sum[:, kv_width:].astype(jnp.bfloat16)],
        axis=1,
    )
    kv_all = lax.all_gather(kv_block, ("row", "seq"), axis=0, tiled=True)
    query_len = queries.shape[0]
    kv_slot = (
        head_first + jnp.arange(head_count, dtype=jnp.int32)
    ) // group_size - col_index * kv_col
    key_sel = jnp.take(kv_all[:, :kv_width].reshape(seq_len, kv_col, HD), kv_slot, axis=1)
    value_sel = jnp.take(kv_all[:, kv_width:].reshape(seq_len, kv_col, HD), kv_slot, axis=1)
    key_pos = jnp.arange(seq_len, dtype=jnp.int32)
    allowed = (key_pos[None, :] <= query_pos[:, None]) & (
        segment_ids[None, :] == jnp.take(segment_ids, query_pos)[:, None]
    )
    query_heads = queries.reshape(query_len, head_count, HD)
    raw_scores = (
        jnp.einsum("qhd,khd->hqk", query_heads, key_sel, preferred_element_type=jnp.float32)
        * score_scale
    )
    capped = softcap * jnp.tanh(raw_scores / softcap)
    weights = jnp.where(allowed[None], jnp.exp(capped), 0.0)
    totals = jnp.sum(weights, axis=2)
    attended = jnp.einsum(
        "hqk,khd->qhd", weights.astype(jnp.bfloat16), value_sel, preferred_element_type=jnp.float32
    )
    attn_out = (
        (attended / totals.T[:, :, None]).astype(jnp.bfloat16).reshape(query_len, head_count * HD)
    )
    out_all = to_rows(attn_out)
    picked = out_all
    branch_sum = lax.psum_scatter(
        jnp.dot(picked, w_out, preferred_element_type=jnp.float32).astype(jnp.bfloat16),
        "col",
        scatter_dimension=0,
        tiled=True,
    ).astype(jnp.float32)
    layer_out = (residual + branch_sum).astype(jnp.bfloat16)
    grad_all = lax.all_gather(out_grad, "col", axis=0, tiled=True)
    grad_wo = jnp.einsum("ln,ld->nd", out_all, grad_all, preferred_element_type=jnp.float32)

    def dout_term(first_row, row_count):
        return jnp.einsum("ld,nd->ln", grad_all, w_out, preferred_element_type=jnp.float32)

    out_heads = to_heads(dout_term, plain_round).reshape(query_len, head_count, HD)
    attn_probs = weights / totals[:, :, None]
    prob_grads = jnp.einsum(
        "qhd,khd->hqk", out_heads, value_sel, preferred_element_type=jnp.float32
    )
    row_dots = jnp.sum(attn_probs * prob_grads, axis=2, keepdims=True)
    grad_scores = (
        attn_probs * (prob_grads - row_dots) * (1.0 - (capped / softcap) ** 2) * score_scale
    ).astype(jnp.bfloat16)
    grad_query = jnp.einsum(
        "hqk,khd->qhd", grad_scores, key_sel, preferred_element_type=jnp.float32
    )
    grad_key_heads = jnp.einsum(
        "hqk,qhd->khd", grad_scores, query_heads, preferred_element_type=jnp.float32
    )
    grad_value_heads = jnp.einsum(
        "hqk,qhd->khd",
        attn_probs.astype(jnp.bfloat16),
        out_heads,
        preferred_element_type=jnp.float32,
    )
    slot_mask = (kv_slot[:, None] == jnp.arange(kv_col, dtype=jnp.int32)[None, :]).astype(
        jnp.float32
    )
    grad_key_part = jnp.sum(
        grad_key_heads[:, :, None, :] * slot_mask[None, :, :, None], axis=1
    ).reshape(seq_len, kv_width)
    grad_value_part = jnp.sum(
        grad_value_heads[:, :, None, :] * slot_mask[None, :, :, None], axis=1
    ).reshape(seq_len, kv_width)
    kv_grad_sum = lax.psum_scatter(
        jnp.concatenate([grad_key_part, grad_value_part], axis=1).astype(jnp.bfloat16),
        ("row", "seq"),
        scatter_dimension=0,
        tiled=True,
    ).astype(jnp.float32)
    cos_block, sin_block = rotary_tables(block_pos, HD)
    grad_key_block = (
        rotate_back(kv_grad_sum[:, :kv_width].reshape(block_len, kv_col, HD), cos_block, sin_block)
        .reshape(block_len, kv_width)
        .astype(jnp.bfloat16)
    )
    kv_grad_block = jnp.concatenate(
        [grad_key_block, kv_grad_sum[:, kv_width:].astype(jnp.bfloat16)], axis=1
    )
    kv_grad_all = lax.all_gather(kv_grad_block, ("row", "seq"), axis=0, tiled=True)
    cos_query, sin_query = rotary_tables(query_pos, HD)
    grad_query_round = (
        rotate_back(grad_query, cos_query, sin_query)
        .reshape(query_len, head_count * HD)
        .astype(jnp.bfloat16)
    )
    grad_query_all = to_rows(grad_query_round)
    grad_wq = jnp.einsum(
        "ld,ln->dn", normed_all, grad_query_all, preferred_element_type=jnp.float32
    )
    grad_wk = jnp.einsum(
        "ld,ln->dn", normed_all, kv_grad_all[:, :kv_width], preferred_element_type=jnp.float32
    )
    grad_wv = jnp.einsum(
        "ld,ln->dn", normed_all, kv_grad_all[:, kv_width:], preferred_element_type=jnp.float32
    )
    total_term = jnp.einsum(
        "ln,dn->ld", grad_query_all, w_query, preferred_element_type=jnp.float32
    )
    total_term = total_term + jnp.einsum(
        "ln,dn->ld", kv_grad_all[:, :kv_width], w_key, preferred_element_type=jnp.float32
    )
    grad_normed = lax.psum_scatter(
        (
            total_term
            + jnp.einsum(
                "ln,dn->ld", kv_grad_all[:, kv_width:], w_value, preferred_element_type=jnp.float32
            )
        ).astype(jnp.bfloat16),
        "col",
        scatter_dimension=0,
        tiled=True,
    ).astype(jnp.float32)
    scaled_grad = grad_normed * norm_gain[None, :]
    total_dot = lax.psum(jnp.sum(scaled_grad * residual, axis=1), ("row", "seq"))
    grad_input = (
        out_grad.astype(jnp.float32)
        + inverse[:, None] * scaled_grad
        - residual * (inverse**3 * total_dot / D)[:, None]
    ).astype(jnp.bfloat16)
    grad_gain = lax.psum(jnp.sum(grad_normed * residual * inverse[:, None], axis=0), "col")
    return (layer_out, grad_input, grad_gain, grad_wq, grad_wk, grad_wv, grad_wo)


VMEM_BYTES = 56 * 1024 * 1024


def remote(source, target, send_sem, recv_sem, place):
    copy = pltpu.make_async_remote_copy(
        src_ref=source,
        dst_ref=target,
        send_sem=send_sem,
        recv_sem=recv_sem,
        device_id=place,
        device_id_type=pl.DeviceIdType.MESH,
    )
    copy.start()
    return copy


def greet(places):
    barrier = pltpu.get_barrier_semaphore()
    for place in places:
        pl.semaphore_signal(
            barrier, inc=1, device_id=place, device_id_type=pl.DeviceIdType.MESH
        )
    pl.semaphore_wait(barrier, len(places))


def neighbours():
    row = lax.axis_index("row")
    seq = lax.axis_index("seq")
    rows = lax.axis_size("row")
    across, core = seq // 2, seq % 2
    plane = [(across, 1 - core), (1 - across, core), (1 - across, 1 - core)]
    plane_ids = [{"row": row, "seq": 2 * a + c} for a, c in plane]
    plane_slots = [2 * c + a for a, c in plane]
    others = [(row + step) % rows for step in range(1, rows)]
    row_ids = [{"row": other, "seq": seq} for other in others]
    return row, across, core, plane_ids, plane_slots, others, row_ids


def reduce_kernel(
    q_part, grads, w_hbm, kv_part, sq_part,
    q_out, o_out, kv_out, sq_out,
    q_rc, o_rc, kv_rc, q_a1, o_a1, kv_a1, q_rx, o_rx, kv_rx, q_a2, o_a2, kv_a2,
    q_rz, o_rz, kv_rz, kv_own, kv_all, sq_send, sq_recv,
    core_send, core_recv, x_send, x_recv, z_send, z_recv, kv_send, kv_recv, sq_ss, sq_rs,
    o_part, w_held, w_sem,
):
    f32, bf16 = jnp.float32, jnp.bfloat16
    w_copy = pltpu.make_async_copy(w_hbm, w_held, w_sem)
    w_copy.start()
    row, across, core, plane_ids, plane_slots, others, row_ids = neighbours()
    rows = len(others) + 1
    core_id, x_id = plane_ids[0], plane_ids[1]
    greet(plane_ids + row_ids)
    seq_len = q_out.shape[0]
    width = q_out.shape[1]
    block = seq_len // 4
    wide = 2 * width
    half_len = seq_len // 2
    pieces = [(None, 0)] + [(0, b) for b in range(4)] + [(1, b) for b in range(4)]
    parts, rcs, a1s = (q_part, o_part), (q_rc, o_rc), (q_a1, o_a1)
    rxs, a2s, rzs, outs = (q_rx, o_rx), (q_a2, o_a2), (q_rz, o_rz), (q_out, o_out)
    core_copies, x_copies, z_copies = [], [], []

    sq_copy = remote(sq_part, sq_recv.at[0], sq_ss.at[0], sq_rs.at[0], core_id)

    def start_core(index):
        which, b = pieces[index]
        copies = []
        if which is None:
            source = kv_part.at[pl.ds(pl.multiple_of((1 - core) * half_len, half_len), half_len)]
            copies.append(
                remote(source, kv_rc, core_send.at[index, 0], core_recv.at[index, 0], core_id)
            )
        else:
            lines = pl.ds(b * block, block)
            for r in range(rows):
                first = pl.multiple_of(r * 2 * wide + (1 - core) * wide, wide)
                copies.append(
                    remote(
                        parts[which].at[lines, pl.ds(first, wide)],
                        rcs[which].at[lines, pl.ds(r * wide, wide)],
                        core_send.at[index, r],
                        core_recv.at[index, r],
                        core_id,
                    )
                )
        core_copies.append(copies)

    for index in range(5):
        start_core(index)

    def output_product():
        w_copy.wait()

        def tile(step, carry):
            first = pl.multiple_of(step * wide, wide)
            o_part[:, pl.ds(first, wide)] = lax.dot_general(
                grads[...],
                w_held[pl.ds(first, wide), :],
                (((1,), (1,)), ((), ())),
                preferred_element_type=f32,
            ).astype(bf16)
            return carry

        lax.fori_loop(0, 2 * rows, tile, 0)
        for index in range(5, len(pieces)):
            start_core(index)

    def core_stage(index):
        which, b = pieces[index]
        for copy in core_copies[index]:
            copy.wait_recv()
        if which is None:
            own = kv_part[pl.ds(pl.multiple_of(core * half_len, half_len), half_len), :]
            kv_a1[...] = (own.astype(f32) + kv_rc[...].astype(f32)).astype(bf16)
            source = kv_a1.at[pl.ds(pl.multiple_of((1 - across) * block, block), block)]
            target = kv_rx
        else:
            lines = pl.ds(b * block, block)
            for r in range(rows):
                for side in range(2):
                    first = pl.multiple_of(r * 2 * wide + core * wide + side * width, width)
                    total = parts[which][lines, pl.ds(first, width)].astype(f32) + rcs[which][
                        lines, pl.ds(r * wide + side * width, width)
                    ].astype(f32)
                    a1s[which][side, lines, pl.ds(r * width, width)] = total.astype(bf16)
            source = a1s[which].at[1 - across, lines]
            target = rxs[which].at[lines]
        x_copies.append(remote(source, target, x_send.at[index], x_recv.at[index], x_id))

    def x_stage(index):
        which, b = pieces[index]
        x_copies[index].wait_recv()
        lines = pl.ds(b * block, block)
        if which is None:
            held = kv_a1[pl.ds(pl.multiple_of(across * block, block), block), :]
            got, kept, landing, span = kv_rx[...], kv_a2, kv_rz, pl.ds(0, block)
        else:
            held = a1s[which][across, lines, :]
            got, kept, landing, span = rxs[which][lines, :], a2s[which], rzs[which], lines
        total = (held.astype(f32) + got.astype(f32)).astype(bf16)
        for r in range(rows):
            kept[r, span, :] = total[:, r * width : (r + 1) * width]
        z_copies.append(
            [
                remote(
                    kept.at[others[step], span],
                    landing.at[step, span],
                    z_send.at[index, step],
                    z_recv.at[index, step],
                    row_ids[step],
                )
                for step in range(rows - 1)
            ]
        )

    def z_stage(index):
        which, b = pieces[index]
        for copy in z_copies[index]:
            copy.wait_recv()
        lines = pl.ds(b * block, block)
        if which is None:
            kept, landing, span = kv_a2, kv_rz, pl.ds(0, block)
        else:
            kept, landing, span = a2s[which], rzs[which], lines
        total = kept[row, span, :].astype(f32)
        for step in range(rows - 1):
            total = total + landing[step, span, :].astype(f32)
        if which is None:
            kv_own[...] = total
            return [
                remote(
                    kv_own, kv_all.at[step], kv_send.at[step], kv_recv.at[step], plane_ids[step]
                )
                for step in range(3)
            ]
        outs[which][lines, :] = total.astype(outs[which].dtype)
        return []

    kv_copies = []
    sq_copies = [sq_copy]
    for turn in range(len(pieces) + 5):
        if turn < len(pieces):
            core_stage(turn)
        if turn == 2:
            output_product()
        if turn == 1:
            sq_copies[0].wait_recv()
            sq_send[0] = sq_part[...] + sq_recv[0]
            sq_copies.append(
                remote(sq_send.at[0], sq_recv.at[1], sq_ss.at[1], sq_rs.at[1], x_id)
            )
        if turn == 3:
            sq_copies[1].wait_recv()
            sq_send[1] = sq_send[0] + sq_recv[1]
            for step in range(rows - 1):
                sq_copies.append(
                    remote(
                        sq_send.at[1],
                        sq_recv.at[2 + step],
                        sq_ss.at[2 + step],
                        sq_rs.at[2 + step],
                        row_ids[step],
                    )
                )
        if 2 <= turn <= len(pieces) + 1:
            x_stage(turn - 2)
        if turn >= 5:
            kv_copies += z_stage(turn - 5)
    total = sq_send[1]
    for step in range(rows - 1):
        sq_copies[2 + step].wait_recv()
        total = total + sq_recv[2 + step]
    sq_out[...] = total
    own_slot = 2 * core + across
    kv_out[pl.ds(pl.multiple_of(own_slot * block, block), block), :] = kv_own[...]
    for step in range(3):
        kv_copies[step].wait_recv()
        first = pl.multiple_of(plane_slots[step] * block, block)
        kv_out[pl.ds(first, block), :] = kv_all[step]
    for copy in sum(core_copies, []) + x_copies + sum(z_copies, []) + kv_copies + sq_copies:
        copy.wait_send()


def reduce_shares(q_part, grads, w_out, kv_part, sq_part, rows):
    f32, bf16 = jnp.float32, jnp.bfloat16
    seq_len, whole = q_part.shape
    width = whole // (4 * rows)
    block = seq_len // 4
    dma = pltpu.SemaphoreType.DMA
    twice = lambda *shape: [pltpu.VMEM(shape, bf16)] * 2
    return pl.pallas_call(
        reduce_kernel,
        out_shape=(
            jax.ShapeDtypeStruct((seq_len, width), f32),
            jax.ShapeDtypeStruct((seq_len, width), bf16),
            jax.ShapeDtypeStruct((seq_len, width), f32),
            jax.ShapeDtypeStruct(sq_part.shape, f32),
        ),
        in_specs=[
            pl.BlockSpec(memory_space=pltpu.VMEM),
            pl.BlockSpec(memory_space=pltpu.VMEM),
            pl.BlockSpec(memory_space=pl.ANY),
            pl.BlockSpec(memory_space=pltpu.VMEM),
            pl.BlockSpec(memory_space=pltpu.VMEM),
        ],
        out_specs=[pl.BlockSpec(memory_space=pltpu.VMEM)] * 4,
        scratch_shapes=[
            *twice(seq_len, whole // 2),
            pltpu.VMEM((seq_len // 2, rows * width), bf16),
            *twice(2, seq_len, rows * width),
            pltpu.VMEM((seq_len // 2, rows * width), bf16),
            *twice(seq_len, rows * width),
            pltpu.VMEM((block, rows * width), bf16),
            *twice(rows, seq_len, width),
            pltpu.VMEM((rows, block, width), bf16),
            *twice(rows - 1, seq_len, width),
            pltpu.VMEM((rows - 1, block, width), bf16),
            pltpu.VMEM((block, width), f32),
            pltpu.VMEM((3, block, width), f32),
            pltpu.VMEM((2, *sq_part.shape), f32),
            pltpu.VMEM((1 + rows, *sq_part.shape), f32),
            dma((9, rows)), dma((9, rows)), dma((9,)), dma((9,)),
            dma((9, rows - 1)), dma((9, rows - 1)), dma((3,)), dma((3,)),
            dma((1 + rows,)), dma((1 + rows,)),
            pltpu.VMEM((seq_len, whole), bf16), pltpu.VMEM(w_out.shape, bf16), dma,
        ],
        compiler_params=pltpu.CompilerParams(
            collective_id=0, has_side_effects=True, vmem_limit_bytes=VMEM_BYTES
        ),
    )(q_part, grads, w_out, kv_part, sq_part)


def gather_kernel(
    q_sum, o_heads, kv_sum, squares, mask, cos_ref, sin_ref, w_hbm,
    a_all, q_all, kv_all, dot_out, branch,
    a_own, q_own, kv_part, q_heads, probs, tanhs, dot_part,
    kv_recv_buf, dot_send, dot_recv,
    z_send, z_recv, x_send, x_recv, core_send, core_recv,
    r_send, r_recv, kz_send, kz_recv, kp_send, kp_recv, dot_ss, dot_rs,
    w_held, w_sem,
):
    f32, bf16 = jnp.float32, jnp.bfloat16
    w_copy = pltpu.make_async_copy(w_hbm, w_held, w_sem)
    w_copy.start()
    row, across, core, plane_ids, plane_slots, others, row_ids = neighbours()
    rows = len(others) + 1
    core_id, x_id = plane_ids[0], plane_ids[1]
    seq_len, width = a_own.shape
    block = seq_len // 4
    wide = 2 * width
    head = width // 2
    own_slot = 2 * core + across
    own_first = pl.multiple_of(row * 2 * wide + own_slot * width, width)
    own_lines = pl.ds(pl.multiple_of(own_slot * block, block), block)
    own_kv = pl.ds(pl.multiple_of(row * width, width), width)
    greet(plane_ids + row_ids)

    def swapped(values):
        return jnp.concatenate([values[:, head // 2 :], values[:, : head // 2]], axis=1)

    def dot(left, right, dims):
        return lax.dot_general(left, right, ((dims[:1], dims[1:]), ((), ())), preferred_element_type=f32)

    score_scale = HD ** (-0.5)
    inverse = jnp.broadcast_to(lax.rsqrt(squares[0:1, :] / D + epsilon), (head, seq_len)).T
    key_raw = kv_sum[:, :head] * inverse
    keys = (key_raw * cos_ref[...] + swapped(key_raw) * sin_ref[...]).astype(bf16)
    values = (kv_sum[:, head:] * inverse).astype(bf16)
    for h in range(2):
        lanes = pl.ds(h * head, head)
        raw = q_sum[:, lanes] * inverse
        query = (raw * cos_ref[...] + swapped(raw) * sin_ref[...]).astype(bf16)
        q_heads[:, lanes] = query
        tanh_scores = jnp.tanh(dot(query, keys, (1, 1)) * (score_scale / softcap))
        weights = jnp.exp(softcap * tanh_scores) * mask[...]
        totals = jnp.sum(weights, axis=1, keepdims=True)
        attended = dot(weights.astype(bf16), values, (1, 0))
        a_own[:, lanes] = (attended / totals).astype(bf16)
        probs[h] = weights / totals
        tanhs[h] = tanh_scores

    pieces = [(which, b) for which in range(2) for b in range(4)]
    owns, alls = (a_own, q_own), (a_all, q_all)
    z_copies, x_copies, core_copies = [], [], []

    def start_z(index):
        which, b = pieces[index]
        lines = pl.ds(b * block, block)
        z_copies.append(
            [
                remote(
                    owns[which].at[lines],
                    alls[which].at[lines, pl.ds(own_first, width)],
                    z_send.at[index, step],
                    z_recv.at[index, step],
                    row_ids[step],
                )
                for step in range(rows - 1)
            ]
        )

    for index in range(3):
        start_z(index)
    a_all[:, pl.ds(own_first, width)] = a_own[...]

    dots = jnp.zeros((seq_len, head), f32)
    grad_key = jnp.zeros((seq_len, head), f32)
    grad_value = jnp.zeros((seq_len, head), f32)
    for h in range(2):
        lanes = pl.ds(h * head, head)
        out_head, query, prob = o_heads[:, lanes], q_heads[:, lanes], probs[h]
        prob_grads = dot(out_head, values, (1, 1))
        row_dots = jnp.sum(prob * prob_grads, axis=1, keepdims=True)
        grad_scores = (
            prob * (prob_grads - row_dots) * (1.0 - tanhs[h] * tanhs[h]) * score_scale
        ).astype(bf16)
        grad_query = dot(grad_scores, keys, (1, 0))
        grad_key = grad_key + dot(grad_scores, query, (0, 0))
        grad_value = grad_value + dot(prob.astype(bf16), out_head, (0, 0))
        dots = dots + grad_query * query.astype(f32)
        q_own[:, lanes] = (
            grad_query * cos_ref[...] - swapped(grad_query) * sin_ref[...]
        ).astype(bf16)
    dots = dots + grad_key * keys.astype(f32) + grad_value * values.astype(f32)
    dot_part[...] = jnp.broadcast_to(jnp.sum(dots.T, axis=0, keepdims=True), dot_part.shape)
    kv_part[:, :head] = grad_key.astype(bf16)
    kv_part[:, head:] = grad_value.astype(bf16)
    q_all[:, pl.ds(own_first, width)] = q_own[...]

    reduces = []
    for step in range(3):
        first = pl.multiple_of(plane_slots[step] * block, block)
        reduces.append(
            remote(
                kv_part.at[pl.ds(first, block)],
                kv_recv_buf.at[step],
                r_send.at[step],
                r_recv.at[step],
                plane_ids[step],
            )
        )
    dot_copies = [
        remote(dot_part, dot_recv.at[step], dot_ss.at[step], dot_rs.at[step], row_ids[step])
        for step in range(rows - 1)
    ]
    def finish_kv():
        total = kv_part[own_lines, :].astype(f32)
        for step in range(3):
            reduces[step].wait_recv()
            total = total + kv_recv_buf[step].astype(f32)
        key_part = total[:, :head]
        key_part = key_part * cos_ref[own_lines, :] - swapped(key_part) * sin_ref[own_lines, :]
        kv_all[own_lines, own_kv] = jnp.concatenate([key_part, total[:, head:]], axis=1).astype(
            bf16
        )
        return [
            remote(
                kv_all.at[own_lines, own_kv],
                kv_all.at[own_lines, own_kv],
                kz_send.at[step],
                kz_recv.at[step],
                row_ids[step],
            )
            for step in range(rows - 1)
        ]

    def x_stage(index):
        which, b = pieces[index]
        lines = pl.ds(b * block, block)
        for copy in z_copies[index]:
            copy.wait_recv()
        if index + 3 < len(pieces):
            start_z(index + 3)
        copies = []
        for r in range(rows):
            first = pl.multiple_of(r * 2 * wide + own_slot * width, width)
            place = alls[which].at[lines, pl.ds(first, width)]
            copies.append(remote(place, place, x_send.at[index, r], x_recv.at[index, r], x_id))
        x_copies.append(copies)

    def core_stage(index):
        which, b = pieces[index]
        lines = pl.ds(b * block, block)
        for copy in x_copies[index]:
            copy.wait_recv()
        copies = []
        for r in range(rows):
            first = pl.multiple_of(r * 2 * wide + core * wide, wide)
            place = alls[which].at[lines, pl.ds(first, wide)]
            copies.append(
                remote(place, place, core_send.at[index, r], core_recv.at[index, r], core_id)
            )
        core_copies.append(copies)

    kv_plane = []
    for turn in range(len(pieces) + 2):
        if turn < len(pieces):
            x_stage(turn)
        if turn == 0:
            total = dot_part[...]
            for step in range(rows - 1):
                dot_copies[step].wait_recv()
                total = total + dot_recv[step]
            dot_send[0] = total
            dot_copies.append(
                remote(
                    dot_send.at[0],
                    dot_recv.at[rows - 1],
                    dot_ss.at[rows - 1],
                    dot_rs.at[rows - 1],
                    x_id,
                )
            )
        if turn == 1:
            kv_z = finish_kv()
        if turn == 4:
            for copy in kv_z:
                copy.wait_recv()
            kv_plane = [
                remote(
                    kv_all.at[own_lines],
                    kv_all.at[own_lines],
                    kp_send.at[step],
                    kp_recv.at[step],
                    plane_ids[step],
                )
                for step in range(3)
            ]
        if turn == 2:
            dot_copies[rows - 1].wait_recv()
            dot_send[1] = dot_send[0] + dot_recv[rows - 1]
            dot_copies.append(
                remote(
                    dot_send.at[1], dot_recv.at[rows], dot_ss.at[rows], dot_rs.at[rows], core_id
                )
            )
        if turn >= 2:
            core_stage(turn - 2)
        if turn == 6:
            w_copy.wait()
        if 6 <= turn <= 9:
            for copy in core_copies[turn - 6]:
                copy.wait_recv()
            lines = pl.ds((turn - 6) * block, block)
            branch[lines, :] = dot(a_all[lines, :], w_held[...], (1, 0)).astype(bf16)
    dot_copies[rows].wait_recv()
    dot_out[...] = dot_send[1] + dot_recv[rows]
    for copy in kv_plane + sum(core_copies[4:], []):
        copy.wait_recv()
    for copy in (
        sum(z_copies + x_copies + core_copies, []) + reduces + kv_z + kv_plane + dot_copies
    ):
        copy.wait_send()


def attend_and_gather(q_sum, o_heads, kv_sum, squares, mask, cosines, sines, w_out, rows):
    f32, bf16 = jnp.float32, jnp.bfloat16
    seq_len, width = q_sum.shape
    block = seq_len // 4
    whole = width * 4 * rows
    dma = pltpu.SemaphoreType.DMA
    return pl.pallas_call(
        gather_kernel,
        out_shape=(
            jax.ShapeDtypeStruct((seq_len, whole), bf16),
            jax.ShapeDtypeStruct((seq_len, whole), bf16),
            jax.ShapeDtypeStruct((seq_len, rows * width), bf16),
            jax.ShapeDtypeStruct(squares.shape, f32),
            jax.ShapeDtypeStruct((seq_len, w_out.shape[1]), bf16),
        ),
        in_specs=[pl.BlockSpec(memory_space=pltpu.VMEM)] * 7
        + [pl.BlockSpec(memory_space=pl.ANY)],
        out_specs=[pl.BlockSpec(memory_space=pltpu.VMEM)] * 5,
        scratch_shapes=[
            *[pltpu.VMEM((seq_len, width), bf16)] * 4,
            *[pltpu.VMEM((2, seq_len, seq_len), f32)] * 2,
            pltpu.VMEM(squares.shape, f32),
            pltpu.VMEM((3, block, width), bf16),
            pltpu.VMEM((2, *squares.shape), f32),
            pltpu.VMEM((rows + 1, *squares.shape), f32),
            dma((8, rows - 1)), dma((8, rows - 1)), dma((8, rows)), dma((8, rows)),
            dma((8, rows)), dma((8, rows)), dma((3,)), dma((3,)),
            dma((rows - 1,)), dma((rows - 1,)), dma((3,)), dma((3,)),
            dma((rows + 1,)), dma((rows + 1,)),
            pltpu.VMEM(w_out.shape, bf16), dma,
        ],
        compiler_params=pltpu.CompilerParams(
            collective_id=1, has_side_effects=True, vmem_limit_bytes=VMEM_BYTES
        ),
    )(q_sum, o_heads, kv_sum, squares, mask, cosines, sines, w_out)


def fast_device(
    motion_ids,
    audio_ids,
    segment_ids,
    motion_table,
    audio_table,
    norm_gain,
    w_query,
    w_key,
    w_value,
    w_out,
    out_grad,
):
    f32, bf16 = jnp.float32, jnp.bfloat16
    seq_len = segment_ids.shape[0]
    row_devices = lax.axis_size("row")
    col_index = lax.axis_index("col")
    own_len = out_grad.shape[0]
    model_width = out_grad.shape[1]
    kv_width = w_key.shape[1]

    swap = [(0, 1), (1, 0)]

    def both_cols(own, other):
        return jnp.concatenate(
            [jnp.where(col_index == 0, own, other), jnp.where(col_index == 0, other, own)], axis=0
        )

    grad_all = both_cols(out_grad, lax.ppermute(out_grad, "col", swap))
    ids = jnp.stack([motion_ids, audio_ids], axis=1)
    ids_all = both_cols(ids, lax.ppermute(ids, "col", swap))
    embedded_all = (
        motion_table.at[ids_all[:, 0]].get(mode="promise_in_bounds").astype(f32)
        + audio_table.at[ids_all[:, 1]].get(mode="promise_in_bounds").astype(f32)
    ).astype(bf16)
    residual_all = embedded_all.astype(f32)
    scaled = (residual_all * norm_gain[None, :]).astype(bf16)

    def product(left, right):
        return jnp.dot(left, right, preferred_element_type=f32).astype(bf16)

    def as_rows(vector):
        return jnp.broadcast_to(vector[None, :], (8, seq_len))

    kv_part = jnp.concatenate(
        [
            product(scaled, w_key).reshape(seq_len, row_devices, HD),
            product(scaled, w_value).reshape(seq_len, row_devices, HD),
        ],
        axis=2,
    ).reshape(seq_len, 2 * kv_width)
    query_sum, out_heads, kv_sum, squares = reduce_shares(
        product(scaled, w_query),
        grad_all,
        w_out,
        kv_part,
        as_rows(jnp.sum(residual_all * residual_all, axis=1)),
        row_devices,
    )
    inverse = lax.rsqrt(squares[0] / D + epsilon)
    positions = jnp.arange(seq_len, dtype=jnp.int32)
    cosines, sines = rotary_tables(positions, HD)
    allowed = (positions[None, :] <= positions[:, None]) & (
        segment_ids[None, :] == segment_ids[:, None]
    )
    out_all, grad_query_all, kv_grad_all, dot_sum, branch_part = attend_and_gather(
        query_sum,
        out_heads,
        kv_sum,
        squares,
        allowed.astype(f32),
        jnp.concatenate([cosines, cosines], axis=1),
        jnp.concatenate([-sines, sines], axis=1),
        w_out,
        row_devices,
    )
    grad_key_all, grad_value_all = (
        jnp.concatenate(
            [kv_grad_all[:, at : at + HD] for at in range(first, 2 * kv_width, 2 * HD)], axis=1
        )
        for first in (0, HD)
    )

    normed = (residual_all * inverse[:, None] * norm_gain[None, :]).astype(bf16)
    grad_wo = jnp.einsum("ln,ld->nd", out_all, grad_all, preferred_element_type=f32)
    grad_wq = jnp.einsum("ld,ln->dn", normed, grad_query_all, preferred_element_type=f32)
    grad_wk = jnp.einsum("ld,ln->dn", normed, grad_key_all, preferred_element_type=f32)
    grad_wv = jnp.einsum("ld,ln->dn", normed, grad_value_all, preferred_element_type=f32)
    normed_part = (
        jnp.einsum("ln,dn->ld", grad_query_all, w_query, preferred_element_type=f32)
        + jnp.einsum("ln,dn->ld", grad_key_all, w_key, preferred_element_type=f32)
        + jnp.einsum("ln,dn->ld", grad_value_all, w_value, preferred_element_type=f32)
    )
    gain_part = jnp.sum(normed_part * residual_all * inverse[:, None], axis=0)
    branch_sum, grad_normed = (
        lax.psum_scatter(
            jnp.concatenate([branch_part, normed_part.astype(bf16)], axis=1),
            "col",
            scatter_dimension=0,
            tiled=True,
        )
        .astype(f32)
        .reshape(own_len, 2, model_width)
        .swapaxes(0, 1)
    )
    sums = jnp.concatenate([gain_part, dot_sum[0]])
    sums = sums + lax.ppermute(sums, "col", swap)
    grad_gain, dot_sum = sums[:model_width], sums[model_width:]

    def own_part(array):
        return lax.dynamic_slice_in_dim(array, col_index * own_len, own_len, axis=0)

    residual = own_part(residual_all)
    inverse_own = own_part(inverse)[:, None]
    layer_out = (residual + branch_sum).astype(bf16)
    grad_input = (
        out_grad.astype(f32)
        + inverse_own * (grad_normed * norm_gain[None, :])
        - residual * (inverse_own**2 * own_part(dot_sum)[:, None] / D)
    ).astype(bf16)
    return (layer_out, grad_input, grad_gain, grad_wq, grad_wk, grad_wv, grad_wo)


def solution(mesh):
    placed = (
        P("col"),
        P("col"),
        P(),
        P(None, ("row", "seq")),
        P(None, ("row", "seq")),
        P(("row", "seq")),
        P(("row", "seq"), "col"),
        P(("row", "seq"), "col"),
        P(("row", "seq"), "col"),
        P("col", ("row", "seq")),
        P("col", ("row", "seq")),
    )
    groups = mesh.shape["row"] * mesh.shape["seq"]
    heads_col = H // mesh.shape["col"]
    whole_heads = (
        heads_col == 2 * groups
        and KV // mesh.shape["col"] == mesh.shape["row"]
        and mesh.shape["seq"] == 4
    )
    return jax.shard_map(
        fast_device if whole_heads else general_device,
        mesh=mesh,
        in_specs=placed,
        out_specs=(
            P("col", ("row", "seq")),
            P("col", ("row", "seq")),
            P(("row", "seq")),
            P(("row", "seq"), "col"),
            P(("row", "seq"), "col"),
            P(("row", "seq"), "col"),
            P("col", ("row", "seq")),
        ),
        check_vma=False,
    )
```
